256 devices in a mesh: lon: 16 (over y, x_lo, core), lat: 16 (over x_hi, z).
Axes of the slice: x: 4 (x_hi: 2, x_lo: 2; x = x_hi * 2 + x_lo), y: 4, z: 8, core: 2. Of those that a mesh axis runs over, the one named last changes fastest.
Arguments:
- state: float32 [16, 16, 256, 512], P('lon', 'lat'), may hold values from -6 to 6
- cotangent: float32 [16, 16, 256, 512], P('lon', 'lat'), may hold values from -6 to 6
- gains: float32 [2, 512], replicated, may hold values from -3 to 3
- senders: int32 [16, 16, 4, 4], P('lon', 'lat'), may hold values from 0 to 7
- halo_map: int32 [16, 16, 4, 1], P('lon', 'lat'), may hold values from 0 to 3
- edge_in: bfloat16 [2, 1024, 512], replicated, may hold values from -0.1875 to 0.1875
- edge_out: bfloat16 [2, 512, 512], replicated, may hold values from -0.25 to 0.25
- node_in: bfloat16 [2, 1024, 512], replicated, may hold values from -0.1875 to 0.1875
- node_out: bfloat16 [2, 512, 512], replicated, may hold values from -0.25 to 0.25
Outputs:
- result: float32 [16, 16, 256, 512], P('lon', 'lat')
- grad_state: float32 [16, 16, 256, 512], P('lon', 'lat')
- grad_gains: float32 [2, 512], replicated
The draws below stay inside these ranges and needn't reach their ends.
All inputs are finite; a program needn't handle non-finite values.
Results may differ from the reference program's by a relative error of at most 0.025.
Values may be sent and summed in bfloat16 or wider, within the bound.
A program may use at most 64 MiB of HBM per device.

```python
import jax
import jax.numpy as jnp
from jax import lax

D = 512
NBLK = 4
BLOCK = 64
K = 4
HB = 1
LAYERS = 2
NODES = 256
SOURCES = 8
N_LON = 16
N_LAT = 16


def touch_ends(drawn, own_key, smallest, top_value):
    shape = drawn.shape
    index_at = [jax.random.randint(jax.random.fold_in(own_key, axis), (), 0, shape[axis]) for axis in range(len(shape))]
    drawn = drawn.at[tuple(index_at)].set(smallest)
    longest = shape.index(max(shape))
    index_at[longest] = (index_at[longest] + 1) % shape[longest]
    return drawn.at[tuple(index_at)].set(top_value)


def level_of(key, extent, split, low, high):
    loudness, own = 1.0, jax.random.fold_in(key, 6)
    for dim, blocks in split:
        draws = jnp.exp(jax.random.uniform(jax.random.fold_in(own, dim), (blocks,), jnp.float32, low / len(split), high / len(split)))
        loudness = loudness * jnp.repeat(draws, extent[dim] // blocks).reshape([-1 if axis == dim else 1 for axis in range(len(extent))])
    return loudness


def bell_draw(own_key, extent, width, limit, shards=(), kind=jnp.bfloat16):
    entries = width * jax.random.normal(own_key, extent, jnp.float32)
    if shards:
        entries = entries * level_of(own_key, extent, shards, -0.22, 0.18)
    return jnp.clip(entries, -limit, limit).astype(kind)


def setup_inputs(seed: int = 0) -> dict:
    arg_keys = jax.random.split(jax.random.key(seed), 10)
    state = bell_draw(arg_keys[0], (N_LON, N_LAT, NODES, D), 1.0, 6.0, ((0, 16), (1, 16)), jnp.float32)
    cotangent = bell_draw(arg_keys[1], (N_LON, N_LAT, NODES, D), 1.0, 6.0, ((0, 16), (1, 16)), jnp.float32)
    gains = bell_draw(arg_keys[2], (LAYERS, D), 0.3, 3.0, (), jnp.float32)
    senders = touch_ends(jax.random.randint(arg_keys[3], (N_LON, N_LAT, NBLK, K), 0, SOURCES), jax.random.fold_in(arg_keys[3], 1), 0, SOURCES - 1).astype(jnp.int32)
    halo_map = touch_ends(jax.random.randint(arg_keys[4], (N_LON, N_LAT, 4, HB), 0, NBLK), jax.random.fold_in(arg_keys[4], 1), 0, NBLK - 1).astype(jnp.int32)
    edge_in = bell_draw(arg_keys[5], (LAYERS, 2 * D, D), (2 * D) ** -0.5, 0.1875)
    edge_out = bell_draw(arg_keys[6], (LAYERS, D, D), D ** -0.5, 0.25)
    node_in = bell_draw(arg_keys[7], (LAYERS, 2 * D, D), (2 * D) ** -0.5, 0.1875)
    node_out = bell_draw(arg_keys[8], (LAYERS, D, D), D ** -0.5, 0.25)
    return {"state": state, "cotangent": cotangent, "gains": gains, "senders": senders, "halo_map": halo_map, "edge_in": edge_in, "edge_out": edge_out, "node_in": node_in, "node_out": node_out}


def rms_scale(rows, gain):
    mean_sq = lax.optimization_barrier(jnp.mean(rows * rows, axis=-1, keepdims=True))
    return (rows * jax.lax.rsqrt(mean_sq + 1e-06) * (1.0 + gain)).astype(jnp.bfloat16)

def layer_step(state, gain, first_edge, second_edge, first_node, second_node, senders, halo_map):
    lon_count, lat_count = (state.shape[0], state.shape[1])
    blocks = state.reshape(lon_count, lat_count, NBLK, BLOCK, D)
    normed = rms_scale(blocks, gain)
    picks = halo_map.reshape(lon_count, lat_count, 4 * HB, 1, 1).astype(jnp.int32)
    sent = jnp.take_along_axis(normed, picks, axis=2).reshape(lon_count, lat_count, 4, HB, BLOCK, D)
    zero_rim = jnp.zeros_like(sent[:, :1, 0])
    from_west = jnp.roll(sent[:, :, 0], 1, axis=0)
    from_east = jnp.roll(sent[:, :, 1], -1, axis=0)
    from_south = jnp.concatenate([zero_rim, sent[:, :-1, 2]], axis=1)
    from_north = jnp.concatenate([sent[:, 1:, 3], zero_rim], axis=1)
    sources = jnp.concatenate([normed, from_west, from_east, from_south, from_north], axis=2)
    project_src = jnp.dot(sources, first_edge[:D], preferred_element_type=jnp.float32)
    project_dst = jnp.dot(normed, first_edge[D:], preferred_element_type=jnp.float32)
    links = senders.reshape(lon_count, lat_count, NBLK * K, 1, 1).astype(jnp.int32)
    chosen = jnp.take_along_axis(project_src, links, axis=2)
    pre = chosen.reshape(lon_count, lat_count, NBLK, K, BLOCK, D) + project_dst[:, :, :, None]
    edges = jax.nn.silu(pre).astype(jnp.bfloat16)
    messages = jnp.dot(edges, second_edge, preferred_element_type=jnp.float32)
    total = lax.optimization_barrier(jnp.sum(messages, axis=3)).astype(jnp.bfloat16)
    inner = jnp.dot(normed, first_node[:D], preferred_element_type=jnp.float32)
    inner = inner + jnp.dot(total, first_node[D:], preferred_element_type=jnp.float32)
    update = jnp.dot(jax.nn.silu(inner).astype(jnp.bfloat16), second_node, preferred_element_type=jnp.float32)
    return (blocks + update).reshape(state.shape)

def reference(state, cotangent, gains, senders, halo_map, edge_in, edge_out, node_in, node_out):

    def forward(current, gain_all):
        for layer in range(LAYERS):
            current = layer_step(current, gain_all[layer], edge_in[layer], edge_out[layer], node_in[layer], node_out[layer], senders, halo_map)
        return current
    result, undo = jax.vjp(forward, state, gains)
    grad_state, grad_gains = undo(cotangent)
    return (result, grad_state, grad_gains)
```

```python
import jax
import jax.numpy as jnp
from jax import lax
from jax.experimental import pallas as pl
from jax.experimental.pallas import tpu as pltpu
from jax.sharding import PartitionSpec as P

MESH = pl.DeviceIdType.MESH
F32 = jnp.float32
BF16 = jnp.bfloat16
LAYERS = 2
NBLK = 4
SLOTS = 4
BLOCK = 64
WIDTH = 512
NODES = NBLK * BLOCK
EDGES = NBLK * SLOTS
EPS = 1e-06


def dot(a, b):
    return jnp.dot(a, b, preferred_element_type=F32)


def dot_t(a, b):
    return lax.dot_general(a, b, (((1,), (1,)), ((), ())), preferred_element_type=F32)


def same(a, b):
    apart = a - b
    return 1 - jnp.minimum(apart * apart, 1)


def sigmoid(v):
    return 0.5 * jnp.tanh(0.5 * v) + 0.5


def kernel(
    n_lon, n_lat,
    state, cotangent, gains, senders, picks, edge_in, edge_out, node_in, node_out,
    result, grad_state, grad_gains,
    x, grad, gain, send_ids, pick_ids, w_ei, w_eo, w_ni, w_no,
    xhat, scale, xhat16, normed, outgoing, arrived, normed_far, p_src, p_own,
    slope_edge, slope_node, edge_sum, hidden, total, d_inner, d_total, d_edge,
    chain, d_dst, d_src, back, returned, d_normed,
    gain_mine, gather_lon, gather_lat, gain_out,
    load_sem, weight_sem, out_sem, send_sem, recv_sem, ar_send, ar_recv,
):
    i = lax.axis_index("lon")
    j = lax.axis_index("lat")
    east, west = lax.rem(i + 1, n_lon), lax.rem(i + n_lon - 1, n_lon)
    north, south = lax.rem(j + 1, n_lat), lax.rem(j + n_lat - 1, n_lat)
    ahead = ((east, j), (west, j), (i, north), (i, south))
    behind = ((west, j), (east, j), (i, south), (i, north))
    has_ahead = (None, None, j < n_lat - 1, j > 0)
    has_behind = (None, None, j > 0, j < n_lat - 1)

    barrier = pltpu.get_barrier_semaphore()

    def greet_lon(t, c):
        pl.semaphore_signal(barrier, inc=1, device_id=(lax.rem(i + t, n_lon), j), device_id_type=MESH)
        return c

    def greet_lat(t, c):
        pl.semaphore_signal(barrier, inc=1, device_id=(i, lax.rem(j + t, n_lat)), device_id_type=MESH)
        return c

    lax.fori_loop(1, n_lon, greet_lon, 0)
    lax.fori_loop(1, n_lat, greet_lat, 0)

    loads = [
        pltpu.make_async_copy(state, x.at[0], load_sem.at[0]),
        pltpu.make_async_copy(gains, gain, load_sem.at[1]),
        pltpu.make_async_copy(picks, pick_ids, load_sem.at[2]),
        pltpu.make_async_copy(senders, send_ids, load_sem.at[3]),
        pltpu.make_async_copy(cotangent, grad, load_sem.at[4]),
    ]
    weights = [
        [
            pltpu.make_async_copy(full.at[layer], held.at[layer], weight_sem.at[layer, n])
            for n, (full, held) in enumerate(
                ((edge_in, w_ei), (node_in, w_ni), (edge_out, w_eo), (node_out, w_no))
            )
        ]
        for layer in range(LAYERS)
    ]
    for copy in loads[:4]:
        copy.start()
    for layer in range(LAYERS):
        for copy in weights[layer]:
            copy.start()
    loads[4].start()

    def guarded(when, action):
        if when is None:
            action()
        else:
            pl.when(when)(action)

    def halo(phase, d, src, dst, device):
        return pltpu.make_async_remote_copy(
            src_ref=src, dst_ref=dst,
            send_sem=send_sem.at[phase, d], recv_sem=recv_sem.at[phase, d],
            device_id=device, device_id_type=MESH,
        )

    zero_block = jnp.zeros((BLOCK, WIDTH), BF16)

    def clear(buffer, phase, d):
        buffer[phase, d] = zero_block

    for copy in loads[:4]:
        copy.wait()
    picked = [pick_ids[0, d] for d in range(4)]
    links = [send_ids[e // SLOTS, e % SLOTS] for e in range(EDGES)]

    earlier = []
    for e in range(EDGES):
        found = jnp.int32(EDGES)
        for f in range(e):
            found = found + same(links[f], links[e]) * (f - found)
        earlier.append(found)
    last = []
    for s in range(2 * NBLK):
        found = jnp.int32(EDGES)
        for f in range(EDGES):
            found = found + same(links[f], s) * (f - found)
        last.append(found)

    for layer in range(LAYERS):
        phase = layer
        one_gain = 1.0 + gain[layer : layer + 1, :]

        def norm_rows(c, carry):
            rows = pl.ds(pl.multiple_of(c * 32, 32), 32)
            v = x[layer, rows, :]
            r = lax.rsqrt(jnp.mean(v * v, axis=-1, keepdims=True) + EPS)
            h = v * r
            xhat[layer, rows, :] = h
            scale[layer, rows, :] = jnp.broadcast_to(r, (32, 128))
            xhat16[c // 2, pl.ds(pl.multiple_of((c % 2) * 32, 32), 32), :] = h.astype(BF16)
            normed[rows, :] = (h * one_gain).astype(BF16)
            return carry

        lax.fori_loop(0, NODES // 32, norm_rows, 0)
        for d in range(4):
            outgoing[phase, d] = xhat16[picked[d]]
        if layer == 0:
            pl.semaphore_wait(barrier, n_lon + n_lat - 2)
        sends = [halo(phase, d, outgoing.at[phase, d], arrived.at[phase, d], ahead[d]) for d in range(4)]
        for d in range(4):
            guarded(has_ahead[d], sends[d].start)

        weights[layer][0].wait()
        own = normed[...]
        p_src[0:NBLK] = dot(own, w_ei[layer, 0:WIDTH, :]).reshape(NBLK, BLOCK, WIDTH)
        p_own[:, 0:WIDTH] = dot(own, w_ei[layer, WIDTH : 2 * WIDTH, :])
        weights[layer][1].wait()
        p_own[:, WIDTH : 2 * WIDTH] = dot(own, w_ni[layer, 0:WIDTH, :])

        for d in range(4):
            guarded(has_behind[d], sends[d].wait_recv)
            if has_behind[d] is not None:
                pl.when(jnp.logical_not(has_behind[d]))(lambda d=d: clear(arrived, phase, d))
        for d in range(4):
            normed_far[d * BLOCK : (d + 1) * BLOCK, :] = (arrived[phase, d].astype(F32) * one_gain).astype(BF16)
        p_src[NBLK : 2 * NBLK] = dot(normed_far[...], w_ei[layer, 0:WIDTH, :]).reshape(NBLK, BLOCK, WIDTH)

        def edge_rows(c, carry):
            start = pl.multiple_of(c * 16, 16)
            for b in range(NBLK):
                to = p_own[pl.ds(b * BLOCK + start, 16), 0:WIDTH]
                acc = jnp.zeros((16, WIDTH), F32)
                for k in range(SLOTS):
                    e = b * SLOTS + k
                    pre = p_src[links[e], pl.ds(start, 16), :] + to
                    s = sigmoid(pre)
                    v = pre * s
                    acc = acc + v
                    slope_edge[layer, e, pl.ds(start, 16), :] = (s + v * (1.0 - s)).astype(BF16)
                edge_sum[pl.ds(b * BLOCK + start, 16), :] = acc.astype(BF16)
            return carry

        lax.fori_loop(0, BLOCK // 16, edge_rows, 0)
        weights[layer][2].wait()
        total[...] = dot(edge_sum[...], w_eo[layer]).astype(BF16)
        inner = dot(total[...], w_ni[layer, WIDTH : 2 * WIDTH, :]) + p_own[:, WIDTH : 2 * WIDTH]
        s = sigmoid(inner)
        v = inner * s
        hidden[...] = v.astype(BF16)
        slope_node[layer] = s + v * (1.0 - s)
        weights[layer][3].wait()
        x[layer + 1] = x[layer] + dot(hidden[...], w_no[layer])
        for d in range(4):
            guarded(has_ahead[d], sends[d].wait_send)

    store_result = pltpu.make_async_copy(x.at[LAYERS], result, out_sem.at[0])
    store_result.start()
    loads[4].wait()
    chain[EDGES] = jnp.zeros((BLOCK, WIDTH), F32)

    for layer in reversed(range(LAYERS)):
        phase = 2 * LAYERS - 1 - layer
        back_phase = phase - LAYERS
        one_gain = 1.0 + gain[layer : layer + 1, :]
        d_inner[...] = (dot_t(grad[...].astype(BF16), w_no[layer]) * slope_node[layer]).astype(BF16)
        d_total[...] = dot_t(d_inner[...], w_ni[layer, WIDTH : 2 * WIDTH, :]).astype(BF16)
        d_edge[...] = dot_t(d_total[...], w_eo[layer])

        def slope_rows(c, carry):
            start = pl.multiple_of(c * 16, 16)
            for b in range(NBLK):
                up = d_edge[pl.ds(b * BLOCK + start, 16), :]
                acc = jnp.zeros((16, WIDTH), F32)
                for k in range(SLOTS):
                    e = b * SLOTS + k
                    d_pre = up * slope_edge[layer, e, pl.ds(start, 16), :].astype(F32)
                    acc = acc + d_pre
                    chain[e, pl.ds(start, 16), :] = d_pre + chain[earlier[e], pl.ds(start, 16), :]
                d_dst[pl.ds(b * BLOCK + start, 16), :] = acc.astype(BF16)
            for s in range(2 * NBLK):
                d_src[pl.ds(s * BLOCK + start, 16), :] = chain[last[s], pl.ds(start, 16), :].astype(BF16)
            return carry

        lax.fori_loop(0, BLOCK // 16, slope_rows, 0)
        far = dot_t(d_src[NODES : 2 * NODES, :], w_ei[layer, 0:WIDTH, :]).astype(BF16)
        for d in range(4):
            back[back_phase, d] = far[d * BLOCK : (d + 1) * BLOCK, :]
        sends = [halo(phase, d, back.at[back_phase, d], returned.at[back_phase, d], behind[d]) for d in range(4)]
        for d in range(4):
            guarded(has_behind[d], sends[d].start)

        d_normed[...] = (
            dot_t(d_inner[...], w_ni[layer, 0:WIDTH, :])
            + dot_t(d_dst[...], w_ei[layer, WIDTH : 2 * WIDTH, :])
            + dot_t(d_src[0:NODES, :], w_ei[layer, 0:WIDTH, :])
        )

        def gain_rows(c, acc):
            rows = pl.ds(pl.multiple_of(c * 16, 16), 16)
            near = d_normed[rows, :] * xhat[layer, rows, :]
            part = pl.ds(pl.multiple_of((c % 4) * 16, 16), 16)
            apart = back[back_phase, c // 4, part, :].astype(F32) * arrived[layer, c // 4, part, :].astype(F32)
            return acc + (near + apart)

        acc = lax.fori_loop(0, NODES // 16, gain_rows, jnp.zeros((16, WIDTH), F32))
        acc = jnp.sum(acc, axis=0, keepdims=True)
        for q in range(4):
            gain_mine[layer * 4 + q : layer * 4 + q + 1, :] = acc[:, q * 128 : (q + 1) * 128]

        if layer == 0:

            def lon_copy(t):
                return pltpu.make_async_remote_copy(
                    src_ref=gain_mine, dst_ref=gather_lon.at[i],
                    send_sem=ar_send.at[0, t], recv_sem=ar_recv.at[0, t],
                    device_id=(lax.rem(i + t, n_lon), j), device_id_type=MESH,
                )

            def lon_start(t, c):
                lon_copy(t).start()
                return c

            lax.fori_loop(1, n_lon, lon_start, 0)
            gather_lon[i] = gain_mine[...]

        for d in range(4):
            guarded(has_ahead[d], sends[d].wait_recv)
            if has_ahead[d] is not None:
                pl.when(jnp.logical_not(has_ahead[d]))(lambda d=d: clear(returned, back_phase, d))

        chosen = [[same(picked[d], b).astype(F32) for d in range(4)] for b in range(NBLK)]

        def norm_back(c, carry):
            start = pl.multiple_of(c * 16, 16)
            sent = [returned[back_phase, d, pl.ds(start, 16), :].astype(F32) for d in range(4)]
            for b in range(NBLK):
                rows = pl.ds(b * BLOCK + start, 16)
                dn = d_normed[rows, :]
                for d in range(4):
                    dn = dn + chosen[b][d] * sent[d]
                dh = dn * one_gain
                h = xhat[layer, rows, :]
                along = jnp.mean(dh * h, axis=-1, keepdims=True)
                r = scale[layer, rows, 0:1]
                grad[rows, :] = grad[rows, :] + r * (dh - h * along)
            return carry

        lax.fori_loop(0, BLOCK // 16, norm_back, 0)
        for d in range(4):
            guarded(has_behind[d], sends[d].wait_send)

    store_grad = pltpu.make_async_copy(grad, grad_state, out_sem.at[1])
    store_grad.start()

    def lon_wait(t, c):
        pltpu.make_async_remote_copy(
            src_ref=gain_mine, dst_ref=gather_lon.at[lax.rem(i + n_lon - t, n_lon)],
            send_sem=ar_send.at[0, t], recv_sem=ar_recv.at[0, t],
            device_id=(lax.rem(i + t, n_lon), j), device_id_type=MESH,
        ).wait()
        return c

    lax.fori_loop(1, n_lon, lon_wait, 0)
    partial_sum = gather_lon[0]
    for t in range(1, n_lon):
        partial_sum = partial_sum + gather_lon[t]
    gain_mine[...] = partial_sum

    def lat_copy(t, slot):
        return pltpu.make_async_remote_copy(
            src_ref=gain_mine, dst_ref=gather_lat.at[slot],
            send_sem=ar_send.at[1, t], recv_sem=ar_recv.at[1, t],
            device_id=(i, lax.rem(j + t, n_lat)), device_id_type=MESH,
        )

    def lat_start(t, c):
        lat_copy(t, j).start()
        return c

    def lat_wait(t, c):
        lat_copy(t, lax.rem(j + n_lat - t, n_lat)).wait()
        return c

    lax.fori_loop(1, n_lat, lat_start, 0)
    gather_lat[j] = partial_sum
    lax.fori_loop(1, n_lat, lat_wait, 0)
    whole = gather_lat[0]
    for t in range(1, n_lat):
        whole = whole + gather_lat[t]
    for layer in range(LAYERS):
        for q in range(4):
            gain_out[layer : layer + 1, q * 128 : (q + 1) * 128] = whole[layer * 4 + q : layer * 4 + q + 1, :]
    store_gain = pltpu.make_async_copy(gain_out, grad_gains, out_sem.at[2])
    store_gain.start()
    store_gain.wait()
    store_grad.wait()
    store_result.wait()


def solution(mesh):
    n_lon, n_lat = mesh.shape["lon"], mesh.shape["lat"]

    def local(state, cotangent, gains, senders, halo_map, edge_in, edge_out, node_in, node_out):
        anywhere = pl.BlockSpec(memory_space=pl.ANY)
        vmem = pltpu.VMEM
        shape = (1, 1, NODES, WIDTH)
        rows = (NODES, WIDTH)
        scratch = [
            vmem((LAYERS + 1,) + rows, F32),
            vmem(rows, F32),
            vmem((LAYERS, WIDTH), F32),
            pltpu.SMEM((NBLK, SLOTS), jnp.int32),
            pltpu.SMEM((1, 4), jnp.int32),
            vmem((LAYERS, 2 * WIDTH, WIDTH), BF16),
            vmem((LAYERS, WIDTH, WIDTH), BF16),
            vmem((LAYERS, 2 * WIDTH, WIDTH), BF16),
            vmem((LAYERS, WIDTH, WIDTH), BF16),
            vmem((LAYERS,) + rows, F32),
            vmem((LAYERS, NODES, 128), F32),
            vmem((NBLK, BLOCK, WIDTH), BF16),
            vmem(rows, BF16),
            vmem((LAYERS, 4, BLOCK, WIDTH), BF16),
            vmem((LAYERS, 4, BLOCK, WIDTH), BF16),
            vmem(rows, BF16),
            vmem((2 * NBLK, BLOCK, WIDTH), F32),
            vmem((NODES, 2 * WIDTH), F32),
            vmem((LAYERS, EDGES, BLOCK, WIDTH), BF16),
            vmem((LAYERS,) + rows, F32),
            vmem(rows, BF16),
            vmem(rows, BF16),
            vmem(rows, BF16),
            vmem(rows, BF16),
            vmem(rows, BF16),
            vmem(rows, F32),
            vmem((EDGES + 1, BLOCK, WIDTH), F32),
            vmem(rows, BF16),
            vmem((2 * NODES, WIDTH), BF16),
            vmem((LAYERS, 4, BLOCK, WIDTH), BF16),
            vmem((LAYERS, 4, BLOCK, WIDTH), BF16),
            vmem(rows, F32),
            vmem((8, 128), F32),
            vmem((n_lon, 8, 128), F32),
            vmem((n_lat, 8, 128), F32),
            vmem((LAYERS, WIDTH), F32),
            pltpu.SemaphoreType.DMA((5,)),
            pltpu.SemaphoreType.DMA((LAYERS, 4)),
            pltpu.SemaphoreType.DMA((3,)),
            pltpu.SemaphoreType.DMA((2 * LAYERS, 4)),
            pltpu.SemaphoreType.DMA((2 * LAYERS, 4)),
            pltpu.SemaphoreType.DMA((2, max(n_lon, n_lat))),
            pltpu.SemaphoreType.DMA((2, max(n_lon, n_lat))),
        ]
        result, grad_state, grad_gains = pl.pallas_call(
            lambda *refs: kernel(n_lon, n_lat, *refs),
            out_shape=(
                jax.ShapeDtypeStruct(rows, F32),
                jax.ShapeDtypeStruct(rows, F32),
                jax.ShapeDtypeStruct((LAYERS, WIDTH), F32),
            ),
            in_specs=[anywhere] * 9,
            out_specs=(anywhere,) * 3,
            scratch_shapes=scratch,
            compiler_params=pltpu.CompilerParams(
                collective_id=0, has_side_effects=True, vmem_limit_bytes=48 * 2**20
            ),
            cost_estimate=pl.CostEstimate(flops=4 * 10**9, bytes_accessed=10**7, transcendentals=2 * 10**6),
            name="mesh_steps",
        )(
            state.reshape(rows),
            cotangent.reshape(rows),
            gains,
            senders.reshape(NBLK, SLOTS),
            halo_map.reshape(1, 4),
            edge_in,
            edge_out,
            node_in,
            node_out,
        )
        return result.reshape(shape), grad_state.reshape(shape), grad_gains

    split = P("lon", "lat", None, None)
    return jax.shard_map(
        local,
        mesh=mesh,
        in_specs=(split, split, P(), split, split, P(), P(), P(), P()),
        out_specs=(split, split, P()),
        check_vma=False,
    )
```

```python
import jax
import jax.numpy as jnp
from jax import lax
from jax.experimental import pallas as pl
from jax.experimental.pallas import tpu as pltpu
from jax.sharding import PartitionSpec as P

MESH = pl.DeviceIdType.MESH
F32 = jnp.float32
BF16 = jnp.bfloat16
LAYERS = 2
NBLK = 4
SLOTS = 4
BLOCK = 64
WIDTH = 512
NODES = NBLK * BLOCK
EDGES = NBLK * SLOTS
EPS = 1e-06


def dot(a, b):
    return jnp.dot(a, b, preferred_element_type=F32)


def dot_t(a, b):
    return lax.dot_general(a, b, (((1,), (1,)), ((), ())), preferred_element_type=F32)


def same(a, b):
    apart = a - b
    return 1 - jnp.minimum(apart * apart, 1)


def sigmoid(v):
    return 0.5 * jnp.tanh(0.5 * v) + 0.5


def kernel(
    n_lon, n_lat,
    state, cotangent, gains, senders, picks, edge_in, edge_out, node_in, node_out,
    result, grad_state, grad_gains,
    x, grad, gain, send_ids, pick_ids, w_ei, w_eo, w_ni, w_no,
    xhat, scale, xhat16, normed, outgoing, arrived, normed_far, p_src, p_own,
    slope_edge, slope_node, edge_sum, hidden, total, d_inner, d_total, d_edge,
    chain, d_dst, d_src, back, returned, d_normed,
    gain_mine, gather_lon, gather_lat, gain_out,
    load_sem, weight_sem, out_sem, send_sem, recv_sem, ar_send, ar_recv,
):
    i = lax.axis_index("lon")
    j = lax.axis_index("lat")
    east, west = lax.rem(i + 1, n_lon), lax.rem(i + n_lon - 1, n_lon)
    north, south = lax.rem(j + 1, n_lat), lax.rem(j + n_lat - 1, n_lat)
    ahead = ((east, j), (west, j), (i, north), (i, south))
    behind = ((west, j), (east, j), (i, south), (i, north))
    has_ahead = (None, None, j < n_lat - 1, j > 0)
    has_behind = (None, None, j > 0, j < n_lat - 1)

    loads = [
        pltpu.make_async_copy(state, x.at[0], load_sem.at[0]),
        pltpu.make_async_copy(gains, gain, load_sem.at[1]),
        pltpu.make_async_copy(picks, pick_ids, load_sem.at[2]),
        pltpu.make_async_copy(senders, send_ids, load_sem.at[3]),
        pltpu.make_async_copy(cotangent, grad, load_sem.at[4]),
    ]
    weights = [
        [
            pltpu.make_async_copy(full.at[layer], held.at[layer], weight_sem.at[layer, n])
            for n, (full, held) in enumerate(
                ((edge_in, w_ei), (node_in, w_ni), (edge_out, w_eo), (node_out, w_no))
            )
        ]
        for layer in range(LAYERS)
    ]
    for copy in loads[:4]:
        copy.start()
    for layer in range(LAYERS):
        for copy in weights[layer]:
            copy.start()
    loads[4].start()

    barrier = pltpu.get_barrier_semaphore()

    def greet_lon(t, c):
        pl.semaphore_signal(barrier, inc=1, device_id=(lax.rem(i + t, n_lon), j), device_id_type=MESH)
        return c

    def greet_lat(t, c):
        pl.semaphore_signal(barrier, inc=1, device_id=(i, lax.rem(j + t, n_lat)), device_id_type=MESH)
        return c

    lax.fori_loop(1, n_lon, greet_lon, 0)
    lax.fori_loop(1, n_lat, greet_lat, 0)

    def guarded(when, action):
        if when is None:
            action()
        else:
            pl.when(when)(action)

    def halo(phase, d, src, dst, device):
        return pltpu.make_async_remote_copy(
            src_ref=src, dst_ref=dst,
            send_sem=send_sem.at[phase, d], recv_sem=recv_sem.at[phase, d],
            device_id=device, device_id_type=MESH,
        )

    zero_block = jnp.zeros((BLOCK, WIDTH), BF16)

    def clear(buffer, phase, d):
        buffer[phase, d] = zero_block

    for copy in loads[:4]:
        copy.wait()
    picked = [pick_ids[0, d] for d in range(4)]
    links = [send_ids[e // SLOTS, e % SLOTS] for e in range(EDGES)]

    earlier = []
    for e in range(EDGES):
        found = jnp.int32(EDGES)
        for f in range(e):
            found = found + same(links[f], links[e]) * (f - found)
        earlier.append(found)
    last = []
    for s in range(2 * NBLK):
        found = jnp.int32(EDGES)
        for f in range(EDGES):
            found = found + same(links[f], s) * (f - found)
        last.append(found)

    for layer in range(LAYERS):
        phase = layer
        one_gain = 1.0 + gain[layer : layer + 1, :]

        def norm_rows(c, carry):
            rows = pl.ds(pl.multiple_of(c * 32, 32), 32)
            v = x[layer, rows, :]
            r = lax.rsqrt(jnp.mean(v * v, axis=-1, keepdims=True) + EPS)
            h = v * r
            xhat[layer, rows, :] = h
            scale[layer, rows, :] = jnp.broadcast_to(r, (32, 128))
            xhat16[c // 2, pl.ds(pl.multiple_of((c % 2) * 32, 32), 32), :] = h.astype(BF16)
            normed[rows, :] = (h * one_gain).astype(BF16)
            return carry

        lax.fori_loop(0, NODES // 32, norm_rows, 0, unroll=True)
        for d in range(4):
            outgoing[phase, d] = xhat16[picked[d]]
        if layer == 0:
            pl.semaphore_wait(barrier, n_lon + n_lat - 2)
        sends = [halo(phase, d, outgoing.at[phase, d], arrived.at[phase, d], ahead[d]) for d in range(4)]
        for d in range(4):
            guarded(has_ahead[d], sends[d].start)

        weights[layer][0].wait()
        own = normed[...]
        p_src[0:NBLK] = dot(own, w_ei[layer, 0:WIDTH, :]).reshape(NBLK, BLOCK, WIDTH)
        p_own[:, 0:WIDTH] = dot(own, w_ei[layer, WIDTH : 2 * WIDTH, :])
        weights[layer][1].wait()
        p_own[:, WIDTH : 2 * WIDTH] = dot(own, w_ni[layer, 0:WIDTH, :])

        for d in range(4):
            guarded(has_behind[d], sends[d].wait_recv)
            if has_behind[d] is not None:
                pl.when(jnp.logical_not(has_behind[d]))(lambda d=d: clear(arrived, phase, d))
        for d in range(4):
            normed_far[d * BLOCK : (d + 1) * BLOCK, :] = (arrived[phase, d].astype(F32) * one_gain).astype(BF16)
        p_src[NBLK : 2 * NBLK] = dot(normed_far[...], w_ei[layer, 0:WIDTH, :]).reshape(NBLK, BLOCK, WIDTH)

        def edge_rows(c, carry):
            start = pl.multiple_of(c * 16, 16)
            for b in range(NBLK):
                to = p_own[pl.ds(b * BLOCK + start, 16), 0:WIDTH]
                acc = jnp.zeros((16, WIDTH), F32)
                for k in range(SLOTS):
                    e = b * SLOTS + k
                    pre = p_src[links[e], pl.ds(start, 16), :] + to
                    s = sigmoid(pre)
                    v = pre * s
                    acc = acc + v
                    slope_edge[layer, e, pl.ds(start, 16), :] = (s + v * (1.0 - s)).astype(BF16)
                edge_sum[pl.ds(b * BLOCK + start, 16), :] = acc.astype(BF16)
            return carry

        lax.fori_loop(0, BLOCK // 16, edge_rows, 0, unroll=2)
        weights[layer][2].wait()
        total[...] = dot(edge_sum[...], w_eo[layer]).astype(BF16)
        inner = dot(total[...], w_ni[layer, WIDTH : 2 * WIDTH, :]) + p_own[:, WIDTH : 2 * WIDTH]
        s = sigmoid(inner)
        v = inner * s
        hidden[...] = v.astype(BF16)
        slope_node[layer] = s + v * (1.0 - s)
        weights[layer][3].wait()
        x[layer + 1] = x[layer] + dot(hidden[...], w_no[layer])
        for d in range(4):
            guarded(has_ahead[d], sends[d].wait_send)

    store_result = pltpu.make_async_copy(x.at[LAYERS], result, out_sem.at[0])
    store_result.start()
    loads[4].wait()
    chain[EDGES] = jnp.zeros((BLOCK, WIDTH), F32)

    for layer in reversed(range(LAYERS)):
        phase = 2 * LAYERS - 1 - layer
        back_phase = phase - LAYERS
        one_gain = 1.0 + gain[layer : layer + 1, :]
        d_inner[...] = (dot_t(grad[...].astype(BF16), w_no[layer]) * slope_node[layer]).astype(BF16)
        d_total[...] = dot_t(d_inner[...], w_ni[layer, WIDTH : 2 * WIDTH, :]).astype(BF16)
        d_edge[...] = dot_t(d_total[...], w_eo[layer])

        def slope_rows(c, carry):
            start = pl.multiple_of(c * 16, 16)
            for b in range(NBLK):
                up = d_edge[pl.ds(b * BLOCK + start, 16), :]
                acc = jnp.zeros((16, WIDTH), F32)
                for k in range(SLOTS):
                    e = b * SLOTS + k
                    d_pre = up * slope_edge[layer, e, pl.ds(start, 16), :].astype(F32)
                    acc = acc + d_pre
                    chain[e, pl.ds(start, 16), :] = d_pre + chain[earlier[e], pl.ds(start, 16), :]
                d_dst[pl.ds(b * BLOCK + start, 16), :] = acc.astype(BF16)
            for s in range(2 * NBLK):
                d_src[pl.ds(s * BLOCK + start, 16), :] = chain[last[s], pl.ds(start, 16), :].astype(BF16)
            return carry

        lax.fori_loop(0, BLOCK // 16, slope_rows, 0, unroll=2)
        far = dot_t(d_src[NODES : 2 * NODES, :], w_ei[layer, 0:WIDTH, :]).astype(BF16)
        for d in range(4):
            back[back_phase, d] = far[d * BLOCK : (d + 1) * BLOCK, :]
        sends = [halo(phase, d, back.at[back_phase, d], returned.at[back_phase, d], behind[d]) for d in range(4)]
        for d in range(4):
            guarded(has_behind[d], sends[d].start)

        d_normed[...] = (
            dot_t(d_inner[...], w_ni[layer, 0:WIDTH, :])
            + dot_t(d_dst[...], w_ei[layer, WIDTH : 2 * WIDTH, :])
            + dot_t(d_src[0:NODES, :], w_ei[layer, 0:WIDTH, :])
        )

        def gain_rows(c, acc):
            rows = pl.ds(pl.multiple_of(c * 16, 16), 16)
            near = d_normed[rows, :] * xhat[layer, rows, :]
            part = pl.ds(pl.multiple_of((c % 4) * 16, 16), 16)
            apart = back[back_phase, c // 4, part, :].astype(F32) * arrived[layer, c // 4, part, :].astype(F32)
            return acc + (near + apart)

        acc = lax.fori_loop(0, NODES // 16, gain_rows, jnp.zeros((16, WIDTH), F32))
        acc = jnp.sum(acc, axis=0, keepdims=True)
        for q in range(4):
            gain_mine[layer * 4 + q : layer * 4 + q + 1, :] = acc[:, q * 128 : (q + 1) * 128]

        if layer == 0:

            def lon_copy(t):
                return pltpu.make_async_remote_copy(
                    src_ref=gain_mine, dst_ref=gather_lon.at[i],
                    send_sem=ar_send.at[0, t], recv_sem=ar_recv.at[0, t],
                    device_id=(lax.rem(i + t, n_lon), j), device_id_type=MESH,
                )

            def lon_start(t, c):
                lon_copy(t).start()
                return c

            lax.fori_loop(1, n_lon, lon_start, 0)
            gather_lon[i] = gain_mine[...]

        for d in range(4):
            guarded(has_ahead[d], sends[d].wait_recv)
            if has_ahead[d] is not None:
                pl.when(jnp.logical_not(has_ahead[d]))(lambda d=d: clear(returned, back_phase, d))

        chosen = [[same(picked[d], b).astype(F32) for d in range(4)] for b in range(NBLK)]

        def norm_back(c, carry):
            start = pl.multiple_of(c * 16, 16)
            sent = [returned[back_phase, d, pl.ds(start, 16), :].astype(F32) for d in range(4)]
            for b in range(NBLK):
                rows = pl.ds(b * BLOCK + start, 16)
                dn = d_normed[rows, :]
                for d in range(4):
                    dn = dn + chosen[b][d] * sent[d]
                dh = dn * one_gain
                h = xhat[layer, rows, :]
                along = jnp.mean(dh * h, axis=-1, keepdims=True)
                r = scale[layer, rows, 0:1]
                grad[rows, :] = grad[rows, :] + r * (dh - h * along)
            return carry

        lax.fori_loop(0, BLOCK // 16, norm_back, 0, unroll=True)
        for d in range(4):
            guarded(has_behind[d], sends[d].wait_send)

    store_grad = pltpu.make_async_copy(grad, grad_state, out_sem.at[1])
    store_grad.start()

    def lon_wait(t, c):
        pltpu.make_async_remote_copy(
            src_ref=gain_mine, dst_ref=gather_lon.at[lax.rem(i + n_lon - t, n_lon)],
            send_sem=ar_send.at[0, t], recv_sem=ar_recv.at[0, t],
            device_id=(lax.rem(i + t, n_lon), j), device_id_type=MESH,
        ).wait()
        return c

    lax.fori_loop(1, n_lon, lon_wait, 0)
    partial_sum = gather_lon[0]
    for t in range(1, n_lon):
        partial_sum = partial_sum + gather_lon[t]
    gain_mine[...] = partial_sum

    def lat_copy(t, slot):
        return pltpu.make_async_remote_copy(
            src_ref=gain_mine, dst_ref=gather_lat.at[slot],
            send_sem=ar_send.at[1, t], recv_sem=ar_recv.at[1, t],
            device_id=(i, lax.rem(j + t, n_lat)), device_id_type=MESH,
        )

    def lat_start(t, c):
        lat_copy(t, j).start()
        return c

    def lat_wait(t, c):
        lat_copy(t, lax.rem(j + n_lat - t, n_lat)).wait()
        return c

    lax.fori_loop(1, n_lat, lat_start, 0)
    gather_lat[j] = partial_sum
    lax.fori_loop(1, n_lat, lat_wait, 0)
    whole = gather_lat[0]
    for t in range(1, n_lat):
        whole = whole + gather_lat[t]
    for layer in range(LAYERS):
        for q in range(4):
            gain_out[layer : layer + 1, q * 128 : (q + 1) * 128] = whole[layer * 4 + q : layer * 4 + q + 1, :]
    store_gain = pltpu.make_async_copy(gain_out, grad_gains, out_sem.at[2])
    store_gain.start()
    store_gain.wait()
    store_grad.wait()
    store_result.wait()


def solution(mesh):
    n_lon, n_lat = mesh.shape["lon"], mesh.shape["lat"]

    def local(state, cotangent, gains, senders, halo_map, edge_in, edge_out, node_in, node_out):
        anywhere = pl.BlockSpec(memory_space=pltpu.HBM)
        vmem = pltpu.VMEM
        shape = (1, 1, NODES, WIDTH)
        rows = (NODES, WIDTH)
        scratch = [
            vmem((LAYERS + 1,) + rows, F32),
            vmem(rows, F32),
            vmem((LAYERS, WIDTH), F32),
            pltpu.SMEM((NBLK, SLOTS), jnp.int32),
            pltpu.SMEM((1, 4), jnp.int32),
            vmem((LAYERS, 2 * WIDTH, WIDTH), BF16),
            vmem((LAYERS, WIDTH, WIDTH), BF16),
            vmem((LAYERS, 2 * WIDTH, WIDTH), BF16),
            vmem((LAYERS, WIDTH, WIDTH), BF16),
            vmem((LAYERS,) + rows, F32),
            vmem((LAYERS, NODES, 128), F32),
            vmem((NBLK, BLOCK, WIDTH), BF16),
            vmem(rows, BF16),
            vmem((LAYERS, 4, BLOCK, WIDTH), BF16),
            vmem((LAYERS, 4, BLOCK, WIDTH), BF16),
            vmem(rows, BF16),
            vmem((2 * NBLK, BLOCK, WIDTH), F32),
            vmem((NODES, 2 * WIDTH), F32),
            vmem((LAYERS, EDGES, BLOCK, WIDTH), BF16),
            vmem((LAYERS,) + rows, F32),
            vmem(rows, BF16),
            vmem(rows, BF16),
            vmem(rows, BF16),
            vmem(rows, BF16),
            vmem(rows, BF16),
            vmem(rows, F32),
            vmem((EDGES + 1, BLOCK, WIDTH), F32),
            vmem(rows, BF16),
            vmem((2 * NODES, WIDTH), BF16),
            vmem((LAYERS, 4, BLOCK, WIDTH), BF16),
            vmem((LAYERS, 4, BLOCK, WIDTH), BF16),
            vmem(rows, F32),
            vmem((8, 128), F32),
            vmem((n_lon, 8, 128), F32),
            vmem((n_lat, 8, 128), F32),
            vmem((LAYERS, WIDTH), F32),
            pltpu.SemaphoreType.DMA((5,)),
            pltpu.SemaphoreType.DMA((LAYERS, 4)),
            pltpu.SemaphoreType.DMA((3,)),
            pltpu.SemaphoreType.DMA((2 * LAYERS, 4)),
            pltpu.SemaphoreType.DMA((2 * LAYERS, 4)),
            pltpu.SemaphoreType.DMA((2, max(n_lon, n_lat))),
            pltpu.SemaphoreType.DMA((2, max(n_lon, n_lat))),
        ]
        result, grad_state, grad_gains = pl.pallas_call(
            lambda *refs: kernel(n_lon, n_lat, *refs),
            out_shape=(
                jax.ShapeDtypeStruct(rows, F32),
                jax.ShapeDtypeStruct(rows, F32),
                jax.ShapeDtypeStruct((LAYERS, WIDTH), F32),
            ),
            in_specs=[anywhere] * 9,
            out_specs=(anywhere,) * 3,
            scratch_shapes=scratch,
            compiler_params=pltpu.CompilerParams(
                collective_id=0, has_side_effects=True, vmem_limit_bytes=60 * 2**20
            ),
            cost_estimate=pl.CostEstimate(flops=4 * 10**9, bytes_accessed=10**7, transcendentals=2 * 10**6),
            name="mesh_steps",
        )(
            state.reshape(rows),
            cotangent.reshape(rows),
            gains,
            senders.reshape(NBLK, SLOTS),
            halo_map.reshape(1, 4),
            edge_in,
            edge_out,
            node_in,
            node_out,
        )
        return result.reshape(shape), grad_state.reshape(shape), grad_gains

    split = P("lon", "lat", None, None)
    return jax.shard_map(
        local,
        mesh=mesh,
        in_specs=(split, split, P(), split, split, P(), P(), P(), P()),
        out_specs=(split, split, P()),
        check_vma=False,
    )
```

```python
import jax
import jax.numpy as jnp
from jax import lax
from jax.experimental import pallas as pl
from jax.experimental.pallas import tpu as pltpu
from jax.sharding import PartitionSpec as P

MESH = pl.DeviceIdType.MESH
F32 = jnp.float32
BF16 = jnp.bfloat16
LAYERS = 2
NBLK = 4
SLOTS = 4
BLOCK = 64
WIDTH = 512
EDGES = NBLK * SLOTS
STREAMS = 2
PART = BLOCK // STREAMS
ROWS = NBLK * PART
CHUNK = 16
EPS = 1e-06


def dot(a, b):
    return jnp.dot(a, b, preferred_element_type=F32)


def same(a, b):
    apart = a - b
    return 1 - jnp.minimum(apart * apart, 1)


def sigmoid(v):
    return 0.5 * jnp.tanh(0.5 * v) + 0.5


def chunks():
    return [pl.ds(c * CHUNK, CHUNK) for c in range(PART // CHUNK)]


def kernel(
    n_lon, n_lat,
    state, cotangent, gains, senders, picks, edge_in, edge_out, node_in, node_out,
    result, grad, grad_gains,
    x, gain, send_ids, pick_ids, w_ei, w_eo, w_ni, w_no, flip_no, flip_total, flip_eo, flip_in,
    xhat, scale, xhat16, normed, outgoing, arrived, normed_far, p_src, p_own,
    slope_edge, slope_node, edge_sum, hidden, total, d_total, d_edge,
    chain, d_own, d_far, back, returned, d_normed,
    gain_mine, gain_near, gather_near, gather_far,
    load_sem, weight_sem, send_sem, recv_sem, ar_send, ar_recv,
):
    i = lax.axis_index("lon")
    j = lax.axis_index("lat")
    east, west = lax.rem(i + 1, n_lon), lax.rem(i + n_lon - 1, n_lon)
    north, south = lax.rem(j + 1, n_lat), lax.rem(j + n_lat - 1, n_lat)
    ahead = ((east, j), (west, j), (i, north), (i, south))
    behind = ((west, j), (east, j), (i, south), (i, north))
    has_ahead = (None, None, j < n_lat - 1, j > 0)
    has_behind = (None, None, j > 0, j < n_lat - 1)

    small = [
        pltpu.make_async_copy(picks, pick_ids, load_sem.at[0]),
        pltpu.make_async_copy(senders, send_ids, load_sem.at[1]),
        pltpu.make_async_copy(gains, gain, load_sem.at[2]),
    ]
    load_x = [
        pltpu.make_async_copy(state.at[:, pl.ds(h * PART, PART), :], x.at[0, h], load_sem.at[3 + h])
        for h in range(STREAMS)
    ]
    load_g = pltpu.make_async_copy(cotangent, grad, load_sem.at[3 + STREAMS])
    weights = [
        [
            pltpu.make_async_copy(full.at[layer], held.at[layer], weight_sem.at[layer, n])
            for n, (full, held) in enumerate(
                ((edge_in, w_ei), (node_in, w_ni), (edge_out, w_eo), (node_out, w_no))
            )
        ]
        for layer in range(LAYERS)
    ]
    for copy in small + load_x:
        copy.start()

    barrier = pltpu.get_barrier_semaphore()

    depth, columns = n_lat // 2, n_lon // 2
    core, column, high, z = i % 2, i // 2, j // depth, j % depth
    near_slot, far_slot = core * depth + z, column * 2 + high
    apart = lambda t, n: min(t, n - t)
    near = [
        (column * 2 + (core + c) % 2, high * depth + (z + t) % depth)
        for t in sorted(range(depth), key=lambda t: -apart(t, depth)) for c in range(2) if c + t > 0
    ]
    far = [
        ((column + t) % columns * 2 + core, (high + c) % 2 * depth + z)
        for c in (1, 0) for t in sorted(range(columns), key=lambda t: -apart(t, columns)) if c + t > 0
    ]
    for device in ahead + tuple(near) + tuple(far):
        pl.semaphore_signal(barrier, inc=1, device_id=device, device_id_type=MESH)
    for layer in range(LAYERS):
        for copy in weights[layer]:
            copy.start()
    load_g.start()

    def guarded(when, action):
        if when is None:
            action()
        else:
            pl.when(when)(action)

    zeros = jnp.zeros((PART, WIDTH), BF16)
    for d in (2, 3):

        def clear_arrived(d=d):
            for layer in range(LAYERS):
                for h in range(STREAMS):
                    arrived[layer, h, d] = zeros

        def clear_returned(d=d):
            for layer in range(LAYERS):
                for h in range(STREAMS):
                    returned[layer, h, d] = zeros

        pl.when(jnp.logical_not(has_behind[d]))(clear_arrived)
        pl.when(jnp.logical_not(has_ahead[d]))(clear_returned)
    chain[EDGES] = jnp.zeros((PART, WIDTH), F32)

    for copy in small:
        copy.wait()
    picked = [pick_ids[0, d] for d in range(4)]
    links = [send_ids[e // SLOTS, e % SLOTS] for e in range(EDGES)]
    chosen = [[same(picked[d], b).astype(F32) for d in range(4)] for b in range(NBLK)]

    earlier = []
    for e in range(EDGES):
        found = jnp.int32(EDGES)
        for f in range(e):
            found = found + same(links[f], links[e]) * (f - found)
        earlier.append(found)
    last = []
    for s in range(2 * NBLK):
        found = jnp.int32(EDGES)
        for f in range(EDGES):
            found = found + same(links[f], s) * (f - found)
        last.append(found)

    one_gain = [None] * LAYERS

    def halo(phase, h, d):
        if phase < LAYERS:
            src, dst, device = outgoing.at[phase, h, d], arrived.at[phase, h, d], ahead[d]
        else:
            layer = 2 * LAYERS - 1 - phase
            src, dst, device = back.at[layer, h, d], returned.at[layer, h, d], behind[d]
        return pltpu.make_async_remote_copy(
            src_ref=src, dst_ref=dst,
            send_sem=send_sem.at[phase, h, d], recv_sem=recv_sem.at[phase, h, d],
            device_id=device, device_id_type=MESH,
        )

    order = (2, 3, 0, 1)

    def start_halo(phase, h):
        for d in order:
            guarded((has_ahead if phase < LAYERS else has_behind)[d], halo(phase, h, d).start)

    def wait_halo(phase, h):
        for d in order:
            guarded((has_behind if phase < LAYERS else has_ahead)[d], halo(phase, h, d).wait_recv)

    def norm(layer, h):
        for b in range(NBLK):
            v = x[layer, h, b]
            r = lax.rsqrt(jnp.mean(v * v, axis=-1, keepdims=True) + EPS)
            unit = v * r
            xhat[layer, h, b] = unit
            scale[layer, h, b] = jnp.broadcast_to(r, (PART, 128))
            xhat16[h, b] = unit.astype(BF16)
            normed[h, b * PART : (b + 1) * PART, :] = (unit * one_gain[layer]).astype(BF16)

    def send(layer, h):
        for d in range(4):
            outgoing[layer, h, d] = xhat16[h, picked[d]]
        start_halo(layer, h)

    def own(layer, h):
        if layer == 0 and h == 0:
            weights[layer][0].wait()
            weights[layer][1].wait()
        rows = normed[h]
        p_src[h, 0:NBLK] = dot(rows, w_ei[layer, 0:WIDTH, :]).reshape(NBLK, PART, WIDTH)
        p_own[h, :, 0:WIDTH] = dot(rows, w_ei[layer, WIDTH : 2 * WIDTH, :])
        p_own[h, :, WIDTH : 2 * WIDTH] = dot(rows, w_ni[layer, 0:WIDTH, :])

    def finish(layer, h):
        wait_halo(layer, h)
        for d in range(4):
            normed_far[h, d * PART : (d + 1) * PART, :] = (
                arrived[layer, h, d].astype(F32) * one_gain[layer]
            ).astype(BF16)
        p_src[h, NBLK : 2 * NBLK] = dot(normed_far[h], w_ei[layer, 0:WIDTH, :]).reshape(NBLK, PART, WIDTH)
        for c, rows in enumerate(chunks()):
            for b in range(NBLK):
                at = pl.ds(b * PART + c * CHUNK, CHUNK)
                to = p_own[h, at, 0:WIDTH]
                acc = None
                for k in range(SLOTS):
                    e = b * SLOTS + k
                    pre = p_src[h, links[e], rows, :] + to
                    s = sigmoid(pre)
                    v = pre * s
                    acc = v if acc is None else acc + v
                    slope_edge[layer, h, e, rows, :] = (s + v * (1.0 - s)).astype(BF16)
                edge_sum[h, at, :] = acc.astype(BF16)
        total[h] = dot(edge_sum[h], w_eo[layer]).astype(BF16)
        inner = dot(total[h], w_ni[layer, WIDTH : 2 * WIDTH, :]) + p_own[h, :, WIDTH : 2 * WIDTH]
        s = sigmoid(inner)
        v = inner * s
        hidden[h] = v.astype(BF16)
        slope_node[layer, h] = s + v * (1.0 - s)
        after = x[layer, h] + dot(hidden[h], w_no[layer]).reshape(NBLK, PART, WIDTH)
        if layer + 1 < LAYERS:
            x[layer + 1, h] = after
        else:
            result[:, pl.ds(h * PART, PART), :] = after

    def flip(layer):
        flip_no[layer] = w_no[layer].T
        flip_total[layer] = w_ni[layer, WIDTH : 2 * WIDTH, :].T
        flip_eo[layer] = w_eo[layer].T
        flip_in[layer, 0:WIDTH, :] = w_ei[layer, 0:WIDTH, :].T
        flip_in[layer, WIDTH : 2 * WIDTH, :] = w_ei[layer, WIDTH : 2 * WIDTH, :].T
        flip_in[layer, 2 * WIDTH : 3 * WIDTH, :] = w_ni[layer, 0:WIDTH, :].T

    def back_far(layer, h):
        g = grad[:, pl.ds(h * PART, PART), :].reshape(ROWS, WIDTH).astype(BF16)
        d_inner = (dot(g, flip_no[layer]) * slope_node[layer, h]).astype(BF16)
        d_own[h, :, 2 * WIDTH : 3 * WIDTH] = d_inner
        d_total[h] = dot(d_inner, flip_total[layer]).astype(BF16)
        d_edge[h] = dot(d_total[h], flip_eo[layer])
        for c, rows in enumerate(chunks()):
            for b in range(NBLK):
                at = pl.ds(b * PART + c * CHUNK, CHUNK)
                up = d_edge[h, at, :]
                acc = None
                for k in range(SLOTS):
                    e = b * SLOTS + k
                    d_pre = up * slope_edge[layer, h, e, rows, :].astype(F32)
                    acc = d_pre if acc is None else acc + d_pre
                    chain[e, rows, :] = d_pre + chain[earlier[e], rows, :]
                d_own[h, at, WIDTH : 2 * WIDTH] = acc.astype(BF16)
            for b in range(NBLK):
                at = pl.ds(b * PART + c * CHUNK, CHUNK)
                d_own[h, at, 0:WIDTH] = chain[last[b], rows, :].astype(BF16)
                d_far[h, at, :] = chain[last[NBLK + b], rows, :].astype(BF16)
        d_halo = dot(d_far[h], flip_in[layer, 0:WIDTH, :]).astype(BF16)
        for d in range(4):
            back[layer, h, d] = d_halo[d * PART : (d + 1) * PART, :]

    def back_own(layer, h):
        d_normed[h] = dot(d_own[h], flip_in[layer]).reshape(NBLK, PART, WIDTH)

    def gain_terms(layer, h):
        acc = None
        for b in range(NBLK):
            for rows in chunks():
                near = d_normed[h, b, rows, :] * xhat[layer, h, b, rows, :]
                apart = back[layer, h, b, rows, :].astype(F32) * arrived[layer, h, b, rows, :].astype(F32)
                acc = near + apart if acc is None else acc + (near + apart)
        return acc

    def keep_gain(layer, acc):
        acc = jnp.sum(acc, axis=0, keepdims=True)
        for q in range(4):
            gain_mine[layer * 4 + q : layer * 4 + q + 1, :] = acc[:, q * 128 : (q + 1) * 128]

    def back_norm(layer, h):
        wait_halo(2 * LAYERS - 1 - layer, h)
        for c, rows in enumerate(chunks()):
            sent = [returned[layer, h, d, rows, :].astype(F32) for d in range(4)]
            for b in range(NBLK):
                dn = d_normed[h, b, rows, :]
                for d in range(4):
                    dn = dn + chosen[b][d] * sent[d]
                dh = dn * one_gain[layer]
                unit = xhat[layer, h, b, rows, :]
                along = jnp.mean(dh * unit, axis=-1, keepdims=True)
                r = scale[layer, h, b, rows, 0:1]
                at = pl.ds(h * PART + c * CHUNK, CHUNK)
                grad[b, at, :] = grad[b, at, :] + r * (dh - unit * along)

    for layer in range(LAYERS):
        one_gain[layer] = 1.0 + gain[layer : layer + 1, :]
    load_x[0].wait()
    norm(0, 0)
    pl.semaphore_wait(barrier, 4 + len(near) + len(far))
    send(0, 0)
    for h in range(1, STREAMS):
        load_x[h].wait()
        norm(0, h)
        send(0, h)
    for h in range(STREAMS):
        own(0, h)
    for copy in weights[0][2:] + weights[1]:
        copy.wait()
    flip(1)
    for layer in range(LAYERS):
        for h in range(STREAMS):
            finish(layer, h)
            if layer + 1 < LAYERS:
                norm(layer + 1, h)
                send(layer + 1, h)
                own(layer + 1, h)
                if h == STREAMS - 1:
                    flip(0)
            else:
                if h == 0:
                    load_g.wait()
                back_far(layer, h)
                start_halo(LAYERS, h)
                back_own(layer, h)

    for layer in reversed(range(LAYERS)):
        terms = None
        if layer == LAYERS - 1:
            for h in range(STREAMS):
                more = gain_terms(layer, h)
                terms = more if terms is None else terms + more
            keep_gain(layer, terms)
            continue
        for h in range(STREAMS):
            back_norm(layer + 1, h)
            back_far(layer, h)
            if layer > 0 or h < STREAMS - 1:
                start_halo(2 * LAYERS - 1 - layer, h)
            back_own(layer, h)
            more = gain_terms(layer, h)
            terms = more if terms is None else terms + more
        keep_gain(layer, terms)

    def near_copy(t):
        return pltpu.make_async_remote_copy(
            src_ref=gain_mine, dst_ref=gather_near.at[near_slot], send_sem=ar_send.at[0], recv_sem=ar_recv.at[0],
            device_id=near[t], device_id_type=MESH,
        )

    def far_copy(t):
        return pltpu.make_async_remote_copy(
            src_ref=gain_near, dst_ref=gather_far.at[far_slot], send_sem=ar_send.at[1], recv_sem=ar_recv.at[1],
            device_id=far[t], device_id_type=MESH,
        )

    def all_of(gather, n, sem):
        return pltpu.make_async_copy(gather.at[pl.ds(0, n)], gather.at[pl.ds(0, n)], sem)

    for t in range(len(near)):
        near_copy(t).start()
    start_halo(2 * LAYERS - 1, STREAMS - 1)
    gather_near[near_slot] = gain_mine[...]

    for h in range(STREAMS - 1):
        back_norm(0, h)
    all_of(gather_near, len(near), ar_recv.at[0]).wait()
    part = gather_near[0]
    for t in range(1, len(near) + 1):
        part = part + gather_near[t]
    gain_near[...] = part
    for t in range(len(far)):
        far_copy(t).start()
    gather_far[far_slot] = part
    back_norm(0, STREAMS - 1)
    for phase in range(2 * LAYERS):
        for h in range(STREAMS):
            for d in range(4):
                guarded((has_ahead if phase < LAYERS else has_behind)[d], halo(phase, h, d).wait_send)
    all_of(gather_near, len(near), ar_send.at[0]).wait()
    all_of(gather_far, len(far), ar_recv.at[1]).wait()
    whole = gather_far[0]
    for t in range(1, len(far) + 1):
        whole = whole + gather_far[t]
    for layer in range(LAYERS):
        for q in range(4):
            grad_gains[layer : layer + 1, q * 128 : (q + 1) * 128] = whole[layer * 4 + q : layer * 4 + q + 1, :]
    all_of(gather_far, len(far), ar_send.at[1]).wait()


def hand_over(result, grad_state, grad_gains, result_out, grad_out, gains_out, sem):
    copies = [pltpu.make_async_copy(grad_gains, gains_out, sem.at[2 * NBLK])]
    for b in range(NBLK):
        copies.append(pltpu.make_async_copy(result.at[b], result_out.at[b], sem.at[b]))
        copies.append(pltpu.make_async_copy(grad_state.at[b], grad_out.at[b], sem.at[NBLK + b]))
    for copy in copies:
        copy.start()
    for copy in copies:
        copy.wait()


def solution(mesh):
    n_lon, n_lat = mesh.shape["lon"], mesh.shape["lat"]

    def local(state, cotangent, gains, senders, halo_map, edge_in, edge_out, node_in, node_out):
        outside = pl.BlockSpec(memory_space=pltpu.HBM)
        vmem = pltpu.VMEM
        whole = (NBLK, BLOCK, WIDTH)
        split_rows = (STREAMS, NBLK, PART, WIDTH)
        flat = (STREAMS, ROWS, WIDTH)
        halos = (LAYERS, STREAMS, 4, PART, WIDTH)
        scratch = [
            vmem((LAYERS,) + split_rows, F32),
            vmem((LAYERS, WIDTH), F32),
            pltpu.SMEM((NBLK, SLOTS), jnp.int32),
            pltpu.SMEM((1, 4), jnp.int32),
            vmem((LAYERS, 2 * WIDTH, WIDTH), BF16),
            vmem((LAYERS, WIDTH, WIDTH), BF16),
            vmem((LAYERS, 2 * WIDTH, WIDTH), BF16),
            vmem((LAYERS, WIDTH, WIDTH), BF16),
            vmem((LAYERS, WIDTH, WIDTH), BF16),
            vmem((LAYERS, WIDTH, WIDTH), BF16),
            vmem((LAYERS, WIDTH, WIDTH), BF16),
            vmem((LAYERS, 3 * WIDTH, WIDTH), BF16),
            vmem((LAYERS,) + split_rows, F32),
            vmem((LAYERS, STREAMS, NBLK, PART, 128), F32),
            vmem(split_rows, BF16),
            vmem(flat, BF16),
            vmem(halos, BF16),
            vmem(halos, BF16),
            vmem(flat, BF16),
            vmem((STREAMS, 2 * NBLK, PART, WIDTH), F32),
            vmem((STREAMS, ROWS, 2 * WIDTH), F32),
            vmem((LAYERS, STREAMS, EDGES, PART, WIDTH), BF16),
            vmem((LAYERS,) + flat, F32),
            vmem(flat, BF16),
            vmem(flat, BF16),
            vmem(flat, BF16),
            vmem(flat, BF16),
            vmem(flat, F32),
            vmem((EDGES + 1, PART, WIDTH), F32),
            vmem((STREAMS, ROWS, 3 * WIDTH), BF16),
            vmem(flat, BF16),
            vmem(halos, BF16),
            vmem(halos, BF16),
            vmem(split_rows, F32),
            vmem((8, 128), F32),
            vmem((8, 128), F32),
            vmem((n_lat, 8, 128), F32),
            vmem((n_lon, 8, 128), F32),
            pltpu.SemaphoreType.DMA((4 + STREAMS,)),
            pltpu.SemaphoreType.DMA((LAYERS, 4)),
            pltpu.SemaphoreType.DMA((2 * LAYERS, STREAMS, 4)),
            pltpu.SemaphoreType.DMA((2 * LAYERS, STREAMS, 4)),
            pltpu.SemaphoreType.DMA((2,)),
            pltpu.SemaphoreType.DMA((2,)),
        ]
        result, grad_state, grad_gains = pl.pallas_call(
            lambda *refs: kernel(n_lon, n_lat, *refs),
            out_shape=(vmem(whole, F32), vmem(whole, F32), vmem((LAYERS, WIDTH), F32)),
            in_specs=[outside] * 9,
            scratch_shapes=scratch,
            compiler_params=pltpu.CompilerParams(
                collective_id=0, has_side_effects=True, vmem_limit_bytes=60 * 2**20
            ),
            cost_estimate=pl.CostEstimate(flops=4 * 10**9, bytes_accessed=10**7, transcendentals=2 * 10**6),
            name="mesh_steps",
        )(
            state.reshape(whole),
            cotangent.reshape(whole),
            gains,
            senders.reshape(NBLK, SLOTS),
            halo_map.reshape(1, 4),
            edge_in,
            edge_out,
            node_in,
            node_out,
        )
        result, grad_state, grad_gains = pl.pallas_call(
            hand_over,
            out_shape=(
                jax.ShapeDtypeStruct(whole, F32),
                jax.ShapeDtypeStruct(whole, F32),
                jax.ShapeDtypeStruct((LAYERS, WIDTH), F32),
            ),
            in_specs=[pl.BlockSpec(memory_space=pl.ANY)] * 3,
            out_specs=(outside,) * 3,
            scratch_shapes=[pltpu.SemaphoreType.DMA((2 * NBLK + 1,))],
            compiler_params=pltpu.CompilerParams(vmem_limit_bytes=2**20),
            name="hand_over",
        )(result, grad_state, grad_gains)
        shape = (1, 1, NBLK * BLOCK, WIDTH)
        return result.reshape(shape), grad_state.reshape(shape), grad_gains

    split = P("lon", "lat", None, None)
    return jax.shard_map(
        local,
        mesh=mesh,
        in_specs=(split, split, P(), split, split, P(), P(), P(), P()),
        out_specs=(split, split, P()),
        check_vma=False,
    )
```

```python
import jax
import jax.numpy as jnp
from jax import lax
from jax.experimental import pallas as pl
from jax.experimental.pallas import tpu as pltpu
from jax.sharding import PartitionSpec as P

MESH = pl.DeviceIdType.MESH
F32 = jnp.float32
BF16 = jnp.bfloat16
LAYERS = 2
NBLK = 4
SLOTS = 4
BLOCK = 64
WIDTH = 512
EDGES = NBLK * SLOTS
STREAMS = 2
PART = BLOCK // STREAMS
ROWS = NBLK * PART
CHUNK = 16
EPS = 1e-06


def dot(a, b):
    return jnp.dot(a, b, preferred_element_type=F32)


def same(a, b):
    apart = a - b
    return 1 - jnp.minimum(apart * apart, 1)


def sigmoid(v):
    return 0.5 * jnp.tanh(0.5 * v) + 0.5


def chunks():
    return [pl.ds(c * CHUNK, CHUNK) for c in range(PART // CHUNK)]


def kernel(
    n_lon, n_lat,
    state, cotangent, gains, senders, picks, edge_in, edge_out, node_in, node_out,
    result, grad, grad_gains,
    x, gain, send_ids, pick_ids, w_ei, w_eo, w_ni, w_no, w_both, flip_no, flip_both, flip_in,
    xhat, scale, xhat16, normed, outgoing, arrived, normed_far, p_src, p_own,
    slope_edge, slope_node, edge_sum, hidden, d_edge,
    chains, d_own, d_far, back, returned, d_normed,
    gain_mine, gain_near, gather_near, gather_far,
    load_sem, weight_sem, send_sem, recv_sem, ar_send, ar_recv,
):
    i = lax.axis_index("lon")
    j = lax.axis_index("lat")
    east, west = lax.rem(i + 1, n_lon), lax.rem(i + n_lon - 1, n_lon)
    north, south = lax.rem(j + 1, n_lat), lax.rem(j + n_lat - 1, n_lat)
    ahead = ((east, j), (west, j), (i, north), (i, south))
    behind = ((west, j), (east, j), (i, south), (i, north))
    has_ahead = (None, None, j < n_lat - 1, j > 0)
    has_behind = (None, None, j > 0, j < n_lat - 1)

    small = [
        pltpu.make_async_copy(picks, pick_ids, load_sem.at[0]),
        pltpu.make_async_copy(senders, send_ids, load_sem.at[1]),
        pltpu.make_async_copy(gains, gain, load_sem.at[2]),
    ]
    load_x = [
        pltpu.make_async_copy(state.at[:, pl.ds(h * PART, PART), :], x.at[0, h], load_sem.at[3 + h])
        for h in range(STREAMS)
    ]
    load_g = pltpu.make_async_copy(cotangent, grad, load_sem.at[3 + STREAMS])
    weights = [
        [
            pltpu.make_async_copy(full.at[layer], held.at[layer], weight_sem.at[layer, n])
            for n, (full, held) in enumerate(
                ((edge_in, w_ei), (node_in, w_ni), (edge_out, w_eo), (node_out, w_no))
            )
        ]
        for layer in range(LAYERS)
    ]
    for copy in small + load_x:
        copy.start()

    barrier = pltpu.get_barrier_semaphore()

    depth, columns = n_lat // 2, n_lon // 2
    core, column, high, z = i % 2, i // 2, j // depth, j % depth
    near_slot, far_slot = core * depth + z, column * 2 + high
    apart = lambda t, n: min(t, n - t)
    near = [
        (column * 2 + (core + c) % 2, high * depth + (z + t) % depth)
        for t in sorted(range(depth), key=lambda t: -apart(t, depth)) for c in range(2) if c + t > 0
    ]
    far = [
        ((column + t) % columns * 2 + core, (high + c) % 2 * depth + z)
        for c in (1, 0) for t in sorted(range(columns), key=lambda t: -apart(t, columns)) if c + t > 0
    ]
    for device in ahead + tuple(near) + tuple(far):
        pl.semaphore_signal(barrier, inc=1, device_id=device, device_id_type=MESH)
    for layer in range(LAYERS):
        for copy in weights[layer]:
            copy.start()
    load_g.start()

    def guarded(when, action):
        if when is None:
            action()
        else:
            pl.when(when)(action)

    for copy in small:
        copy.wait()
    picked = [pick_ids[0, d] for d in range(4)]
    one_gain = [None] * LAYERS

    def halo(phase, h, d):
        if phase < LAYERS:
            src, dst, device = outgoing.at[phase, h, d], arrived.at[phase, h, d], ahead[d]
        else:
            layer = 2 * LAYERS - 1 - phase
            src, dst, device = back.at[layer, h, d], returned.at[layer, h, d], behind[d]
        return pltpu.make_async_remote_copy(
            src_ref=src, dst_ref=dst,
            send_sem=send_sem.at[phase, h, d], recv_sem=recv_sem.at[phase, h, d],
            device_id=device, device_id_type=MESH,
        )

    order = (2, 3, 0, 1)

    def start_halo(phase, h):
        for d in order:
            guarded((has_ahead if phase < LAYERS else has_behind)[d], halo(phase, h, d).start)

    def wait_halo(phase, h):
        for d in order:
            guarded((has_behind if phase < LAYERS else has_ahead)[d], halo(phase, h, d).wait_recv)

    def norm(layer, h):
        for b in range(NBLK):
            v = x[layer, h, b]
            r = lax.rsqrt(jnp.mean(v * v, axis=-1, keepdims=True) + EPS)
            unit = v * r
            xhat[layer, h, b] = unit
            scale[layer, h, b] = jnp.broadcast_to(r, (PART, 128))
            xhat16[h, b] = unit.astype(BF16)
            normed[h, b * PART : (b + 1) * PART, :] = (unit * one_gain[layer]).astype(BF16)

    def send(layer, h):
        for d in range(4):
            outgoing[layer, h, d] = xhat16[h, picked[d]]
        start_halo(layer, h)

    def own(layer, h):
        rows = normed[h]
        p_src[h, 0:NBLK] = dot(rows, w_ei[layer, 0:WIDTH, :]).reshape(NBLK, PART, WIDTH)
        p_own[h, :, 0:WIDTH] = dot(rows, w_ei[layer, WIDTH : 2 * WIDTH, :])
        p_own[h, :, WIDTH : 2 * WIDTH] = dot(rows, w_ni[layer, 0:WIDTH, :])

    def finish(layer, h):
        wait_halo(layer, h)
        for d in range(4):
            normed_far[h, d * PART : (d + 1) * PART, :] = (
                arrived[layer, h, d].astype(F32) * one_gain[layer]
            ).astype(BF16)
        p_src[h, NBLK : 2 * NBLK] = dot(normed_far[h], w_ei[layer, 0:WIDTH, :]).reshape(NBLK, PART, WIDTH)
        for c, rows in enumerate(chunks()):
            for b in range(NBLK):
                at = pl.ds(b * PART + c * CHUNK, CHUNK)
                to = p_own[h, at, 0:WIDTH]
                acc = None
                for k in range(SLOTS):
                    e = b * SLOTS + k
                    pre = p_src[h, links[e], rows, :] + to
                    s = sigmoid(pre)
                    v = pre * s
                    acc = v if acc is None else acc + v
                    slope_edge[layer, h, e, rows, :] = (s + v * (1.0 - s)).astype(BF16)
                edge_sum[h, at, :] = acc.astype(BF16)
        inner = dot(edge_sum[h], w_both[layer]) + p_own[h, :, WIDTH : 2 * WIDTH]
        s = sigmoid(inner)
        v = inner * s
        hidden[h] = v.astype(BF16)
        slope_node[layer, h] = s + v * (1.0 - s)
        after = x[layer, h] + dot(hidden[h], w_no[layer]).reshape(NBLK, PART, WIDTH)
        if layer + 1 < LAYERS:
            x[layer + 1, h] = after
        else:
            result[:, pl.ds(h * PART, PART), :] = after

    def flip(layer):
        flip_no[layer] = w_no[layer].T
        flip_both[layer] = w_both[layer].T
        flip_in[layer, 0:WIDTH, :] = w_ei[layer, 0:WIDTH, :].T
        flip_in[layer, WIDTH : 2 * WIDTH, :] = w_ei[layer, WIDTH : 2 * WIDTH, :].T
        flip_in[layer, 2 * WIDTH : 3 * WIDTH, :] = w_ni[layer, 0:WIDTH, :].T

    def pieces():
        return [
            (chains[2 * c + half], rows, pl.ds(half * (WIDTH // 2), WIDTH // 2))
            for c, rows in enumerate(chunks())
            for half in range(2)
        ]

    def back_far(layer, h):
        g = grad[:, pl.ds(h * PART, PART), :].reshape(ROWS, WIDTH).astype(BF16)
        d_inner = (dot(g, flip_no[layer]) * slope_node[layer, h]).astype(BF16)
        d_own[h, :, 2 * WIDTH : 3 * WIDTH] = d_inner
        d_edge[h] = dot(d_inner, flip_both[layer])
        for b in range(NBLK):
            acc = [None] * len(chains)
            for k in range(SLOTS):
                e = b * SLOTS + k
                for q, (chain, rows, cols) in enumerate(pieces()):
                    at = pl.ds(b * PART + rows.start, CHUNK)
                    d_pre = d_edge[h, at, cols] * slope_edge[layer, h, e, rows, cols].astype(F32)
                    acc[q] = d_pre if k == 0 else acc[q] + d_pre
                    chain[e] = d_pre + chain[earlier[e]]
            for q, (chain, rows, cols) in enumerate(pieces()):
                at = pl.ds(b * PART + rows.start, CHUNK)
                d_own[h, at, pl.ds(WIDTH + cols.start, cols.size)] = acc[q].astype(BF16)
        for b in range(NBLK):
            for chain, rows, cols in pieces():
                at = pl.ds(b * PART + rows.start, CHUNK)
                d_far[h, at, cols] = chain[last[NBLK + b]].astype(BF16)
                d_own[h, at, cols] = chain[last[b]].astype(BF16)
        d_halo = dot(d_far[h], flip_in[layer, 0:WIDTH, :]).astype(BF16)
        for d in range(4):
            back[layer, h, d] = d_halo[d * PART : (d + 1) * PART, :]

    def back_own(layer, h):
        d_normed[h] = dot(d_own[h], flip_in[layer]).reshape(NBLK, PART, WIDTH)

    def gain_terms(layer, h):
        acc = None
        for b in range(NBLK):
            for rows in chunks():
                near = d_normed[h, b, rows, :] * xhat[layer, h, b, rows, :]
                apart = back[layer, h, b, rows, :].astype(F32) * arrived[layer, h, b, rows, :].astype(F32)
                acc = near + apart if acc is None else acc + (near + apart)
        return acc

    def keep_gain(layer, acc):
        acc = jnp.sum(acc, axis=0, keepdims=True)
        for q in range(4):
            gain_mine[layer * 4 + q : layer * 4 + q + 1, :] = acc[:, q * 128 : (q + 1) * 128]

    def back_norm(layer, h):
        wait_halo(2 * LAYERS - 1 - layer, h)
        for c, rows in enumerate(chunks()):
            sent = [returned[layer, h, d, rows, :].astype(F32) for d in range(4)]
            for b in range(NBLK):
                dn = d_normed[h, b, rows, :]
                for d in range(4):
                    dn = dn + chosen[b][d] * sent[d]
                dh = dn * one_gain[layer]
                unit = xhat[layer, h, b, rows, :]
                along = jnp.mean(dh * unit, axis=-1, keepdims=True)
                r = scale[layer, h, b, rows, 0:1]
                at = pl.ds(h * PART + c * CHUNK, CHUNK)
                grad[b, at, :] = grad[b, at, :] + r * (dh - unit * along)

    for layer in range(LAYERS):
        one_gain[layer] = 1.0 + gain[layer : layer + 1, :]
    load_x[0].wait()
    norm(0, 0)
    pl.semaphore_wait(barrier, 4 + len(near) + len(far))
    send(0, 0)
    for h in range(1, STREAMS):
        load_x[h].wait()
        norm(0, h)
        send(0, h)
    for copy in weights[0][:2]:
        copy.wait()
    for h in range(STREAMS):
        own(0, h)

    zeros = jnp.zeros((PART, WIDTH), BF16)
    for d in (2, 3):

        def clear_arrived(d=d):
            for layer in range(LAYERS):
                for h in range(STREAMS):
                    arrived[layer, h, d] = zeros

        def clear_returned(d=d):
            for layer in range(LAYERS):
                for h in range(STREAMS):
                    returned[layer, h, d] = zeros

        pl.when(jnp.logical_not(has_behind[d]))(clear_arrived)
        pl.when(jnp.logical_not(has_ahead[d]))(clear_returned)
    for chain in chains:
        chain[EDGES] = jnp.zeros((CHUNK, WIDTH // 2), F32)

    links = [send_ids[e // SLOTS, e % SLOTS] for e in range(EDGES)]
    chosen = [[same(picked[d], b).astype(F32) for d in range(4)] for b in range(NBLK)]

    earlier = []
    for e in range(EDGES):
        found = jnp.int32(EDGES)
        for f in range(e):
            found = found + same(links[f], links[e]) * (f - found)
        earlier.append(found)
    last = []
    for s in range(2 * NBLK):
        found = jnp.int32(EDGES)
        for f in range(EDGES):
            found = found + same(links[f], s) * (f - found)
        last.append(found)

    for copy in weights[0][2:] + weights[1]:
        copy.wait()
    for layer in range(LAYERS):
        w_both[layer] = dot(w_eo[layer], w_ni[layer, WIDTH : 2 * WIDTH, :]).astype(BF16)
    flip(1)

    for layer in range(LAYERS - 1):
        for h in range(STREAMS):
            finish(layer, h)
            norm(layer + 1, h)
            send(layer + 1, h)
        for h in range(STREAMS):
            own(layer + 1, h)
        flip(layer)
    load_g.wait()
    for h in range(STREAMS):
        finish(LAYERS - 1, h)
        back_far(LAYERS - 1, h)
        start_halo(LAYERS, h)

    for layer in reversed(range(LAYERS)):
        terms = None
        if layer == LAYERS - 1:
            for h in range(STREAMS):
                back_own(layer, h)
                more = gain_terms(layer, h)
                terms = more if terms is None else terms + more
            keep_gain(layer, terms)
            continue
        for h in range(STREAMS):
            back_norm(layer + 1, h)
            back_far(layer, h)
            if layer > 0 or h < STREAMS - 1:
                start_halo(2 * LAYERS - 1 - layer, h)
            back_own(layer, h)
            more = gain_terms(layer, h)
            terms = more if terms is None else terms + more
        keep_gain(layer, terms)

    def near_copy(t):
        return pltpu.make_async_remote_copy(
            src_ref=gain_mine, dst_ref=gather_near.at[near_slot], send_sem=ar_send.at[0], recv_sem=ar_recv.at[0],
            device_id=near[t], device_id_type=MESH,
        )

    def far_copy(t):
        return pltpu.make_async_remote_copy(
            src_ref=gain_near, dst_ref=gather_far.at[far_slot], send_sem=ar_send.at[1], recv_sem=ar_recv.at[1],
            device_id=far[t], device_id_type=MESH,
        )

    def all_of(gather, n, sem):
        return pltpu.make_async_copy(gather.at[pl.ds(0, n)], gather.at[pl.ds(0, n)], sem)

    for t in range(len(near)):
        near_copy(t).start()
    start_halo(2 * LAYERS - 1, STREAMS - 1)
    gather_near[near_slot] = gain_mine[...]

    for h in range(STREAMS - 1):
        back_norm(0, h)
    all_of(gather_near, len(near), ar_recv.at[0]).wait()
    part = gather_near[0]
    for t in range(1, len(near) + 1):
        part = part + gather_near[t]
    gain_near[...] = part
    for t in range(len(far)):
        far_copy(t).start()
    gather_far[far_slot] = part
    back_norm(0, STREAMS - 1)
    for phase in range(2 * LAYERS):
        for h in range(STREAMS):
            for d in range(4):
                guarded((has_ahead if phase < LAYERS else has_behind)[d], halo(phase, h, d).wait_send)
    all_of(gather_near, len(near), ar_send.at[0]).wait()
    all_of(gather_far, len(far), ar_recv.at[1]).wait()
    whole = gather_far[0]
    for t in range(1, len(far) + 1):
        whole = whole + gather_far[t]
    for layer in range(LAYERS):
        for q in range(4):
            grad_gains[layer : layer + 1, q * 128 : (q + 1) * 128] = whole[layer * 4 + q : layer * 4 + q + 1, :]
    all_of(gather_far, len(far), ar_send.at[1]).wait()


def hand_over(result, grad_state, grad_gains, result_out, grad_out, gains_out, sem):
    copies = [pltpu.make_async_copy(grad_gains, gains_out, sem.at[2 * NBLK])]
    for b in range(NBLK):
        copies.append(pltpu.make_async_copy(result.at[b], result_out.at[b], sem.at[b]))
        copies.append(pltpu.make_async_copy(grad_state.at[b], grad_out.at[b], sem.at[NBLK + b]))
    for copy in copies:
        copy.start()
    for copy in copies:
        copy.wait()


def solution(mesh):
    n_lon, n_lat = mesh.shape["lon"], mesh.shape["lat"]

    def local(state, cotangent, gains, senders, halo_map, edge_in, edge_out, node_in, node_out):
        outside = pl.BlockSpec(memory_space=pltpu.HBM)
        vmem = pltpu.VMEM
        whole = (NBLK, BLOCK, WIDTH)
        split_rows = (STREAMS, NBLK, PART, WIDTH)
        flat = (STREAMS, ROWS, WIDTH)
        halos = (LAYERS, STREAMS, 4, PART, WIDTH)
        scratch = [
            vmem((LAYERS,) + split_rows, F32),
            vmem((LAYERS, WIDTH), F32),
            pltpu.SMEM((NBLK, SLOTS), jnp.int32),
            pltpu.SMEM((1, 4), jnp.int32),
            vmem((LAYERS, 2 * WIDTH, WIDTH), BF16),
            vmem((LAYERS, WIDTH, WIDTH), BF16),
            vmem((LAYERS, 2 * WIDTH, WIDTH), BF16),
            vmem((LAYERS, WIDTH, WIDTH), BF16),
            vmem((LAYERS, WIDTH, WIDTH), BF16),
            vmem((LAYERS, WIDTH, WIDTH), BF16),
            vmem((LAYERS, WIDTH, WIDTH), BF16),
            vmem((LAYERS, 3 * WIDTH, WIDTH), BF16),
            vmem((LAYERS,) + split_rows, F32),
            vmem((LAYERS, STREAMS, NBLK, PART, 128), F32),
            vmem(split_rows, BF16),
            vmem(flat, BF16),
            vmem(halos, BF16),
            vmem(halos, BF16),
            vmem(flat, BF16),
            vmem((STREAMS, 2 * NBLK, PART, WIDTH), F32),
            vmem((STREAMS, ROWS, 2 * WIDTH), F32),
            vmem((LAYERS, STREAMS, EDGES, PART, WIDTH), BF16),
            vmem((LAYERS,) + flat, F32),
            vmem(flat, BF16),
            vmem(flat, BF16),
            vmem(flat, F32),
            [vmem((EDGES + 1, CHUNK, WIDTH // 2), F32)] * (2 * (PART // CHUNK)),
            vmem((STREAMS, ROWS, 3 * WIDTH), BF16),
            vmem(flat, BF16),
            vmem(halos, BF16),
            vmem(halos, BF16),
            vmem(split_rows, F32),
            vmem((8, 128), F32),
            vmem((8, 128), F32),
            vmem((n_lat, 8, 128), F32),
            vmem((n_lon, 8, 128), F32),
            pltpu.SemaphoreType.DMA((4 + STREAMS,)),
            pltpu.SemaphoreType.DMA((LAYERS, 4)),
            pltpu.SemaphoreType.DMA((2 * LAYERS, STREAMS, 4)),
            pltpu.SemaphoreType.DMA((2 * LAYERS, STREAMS, 4)),
            pltpu.SemaphoreType.DMA((2,)),
            pltpu.SemaphoreType.DMA((2,)),
        ]
        result, grad_state, grad_gains = pl.pallas_call(
            lambda *refs: kernel(n_lon, n_lat, *refs),
            out_shape=(vmem(whole, F32), vmem(whole, F32), vmem((LAYERS, WIDTH), F32)),
            in_specs=[outside] * 9,
            scratch_shapes=scratch,
            compiler_params=pltpu.CompilerParams(
                collective_id=0, has_side_effects=True, vmem_limit_bytes=60 * 2**20
            ),
            cost_estimate=pl.CostEstimate(flops=4 * 10**9, bytes_accessed=10**7, transcendentals=2 * 10**6),
            name="mesh_steps",
        )(
            state.reshape(whole),
            cotangent.reshape(whole),
            gains,
            senders.reshape(NBLK, SLOTS),
            halo_map.reshape(1, 4),
            edge_in,
            edge_out,
            node_in,
            node_out,
        )
        result, grad_state, grad_gains = pl.pallas_call(
            hand_over,
            out_shape=(
                jax.ShapeDtypeStruct(whole, F32),
                jax.ShapeDtypeStruct(whole, F32),
                jax.ShapeDtypeStruct((LAYERS, WIDTH), F32),
            ),
            in_specs=[pl.BlockSpec(memory_space=pl.ANY)] * 3,
            out_specs=(outside,) * 3,
            scratch_shapes=[pltpu.SemaphoreType.DMA((2 * NBLK + 1,))],
            compiler_params=pltpu.CompilerParams(vmem_limit_bytes=2**20),
            name="hand_over",
        )(result, grad_state, grad_gains)
        shape = (1, 1, NBLK * BLOCK, WIDTH)
        return result.reshape(shape), grad_state.reshape(shape), grad_gains

    split = P("lon", "lat", None, None)
    return jax.shard_map(
        local,
        mesh=mesh,
        in_specs=(split, split, P(), split, split, P(), P(), P(), P()),
        out_specs=(split, split, P()),
        check_vma=False,
    )
```

```python
import jax
import jax.numpy as jnp
from jax import lax
from jax.experimental import pallas as pl
from jax.experimental.pallas import tpu as pltpu
from jax.sharding import PartitionSpec as P

MESH = pl.DeviceIdType.MESH
F32 = jnp.float32
BF16 = jnp.bfloat16
LAYERS = 2
NBLK = 4
SLOTS = 4
BLOCK = 64
WIDTH = 512
EDGES = NBLK * SLOTS
STREAMS = 2
PART = BLOCK // STREAMS
ROWS = NBLK * PART
CHUNK = 16
EPS = 1e-06


def dot(a, b):
    return jnp.dot(a, b, preferred_element_type=F32)


def same(a, b):
    apart = a - b
    return 1 - jnp.minimum(apart * apart, 1)


def silu_of_half(v):
    u = 1.0 + jnp.tanh(v)
    out = v * u
    return out, u + out * (2.0 - u)


def chunks():
    return [pl.ds(c * CHUNK, CHUNK) for c in range(PART // CHUNK)]


def kernel(
    n_lon, n_lat,
    state, cotangent, gains, senders, picks, edge_in, edge_out, node_in, node_out,
    result, grad, grad_gains,
    x, gain, send_ids, pick_ids, w_ei, w_eo, w_ni, w_no, w_both, flip_no, flip_both, flip_in,
    xhat, scale, xhat16, normed, outgoing, arrived, normed_far, p_src, p_own,
    slope_edge, slope_node, edge_sum, hidden, d_hidden, d_edge,
    chains, d_own, d_far, back, returned, d_normed,
    gain_mine, gain_near, gather_near, gather_far,
    load_sem, weight_sem, send_sem, recv_sem, ar_send, ar_recv,
):
    i = lax.axis_index("lon")
    j = lax.axis_index("lat")
    east, west = lax.rem(i + 1, n_lon), lax.rem(i + n_lon - 1, n_lon)
    north, south = lax.rem(j + 1, n_lat), lax.rem(j + n_lat - 1, n_lat)
    ahead = ((east, j), (west, j), (i, north), (i, south))
    behind = ((west, j), (east, j), (i, south), (i, north))
    has_ahead = (None, None, j < n_lat - 1, j > 0)
    has_behind = (None, None, j > 0, j < n_lat - 1)

    small = [
        pltpu.make_async_copy(picks, pick_ids, load_sem.at[0]),
        pltpu.make_async_copy(senders, send_ids, load_sem.at[1]),
        pltpu.make_async_copy(gains, gain, load_sem.at[2]),
    ]
    load_x = [
        pltpu.make_async_copy(state.at[:, pl.ds(h * PART, PART), :], x.at[0, h], load_sem.at[3 + h])
        for h in range(STREAMS)
    ]
    load_g = pltpu.make_async_copy(cotangent, grad, load_sem.at[3 + STREAMS])
    weights = [
        [
            pltpu.make_async_copy(full.at[layer], held.at[layer], weight_sem.at[layer, n])
            for n, (full, held) in enumerate(
                ((edge_in, w_ei), (node_in, w_ni), (edge_out, w_eo), (node_out, w_no))
            )
        ]
        for layer in range(LAYERS)
    ]
    for copy in small + load_x:
        copy.start()

    barrier = pltpu.get_barrier_semaphore()

    depth, columns = n_lat // 2, n_lon // 2
    core, column, high, z = i % 2, i // 2, j // depth, j % depth
    near_slot, far_slot = core * depth + z, column * 2 + high
    apart = lambda t, n: min(t, n - t)
    near = [
        (column * 2 + (core + c) % 2, high * depth + (z + t) % depth)
        for t in sorted(range(depth), key=lambda t: -apart(t, depth)) for c in range(2) if c + t > 0
    ]
    far = [
        ((column + t) % columns * 2 + core, (high + c) % 2 * depth + z)
        for c in (1, 0) for t in sorted(range(columns), key=lambda t: -apart(t, columns)) if c + t > 0
    ]
    for device in ahead + tuple(near) + tuple(far):
        pl.semaphore_signal(barrier, inc=1, device_id=device, device_id_type=MESH)
    for layer in range(LAYERS):
        for copy in weights[layer]:
            copy.start()
    load_g.start()

    def guarded(when, action):
        if when is None:
            action()
        else:
            pl.when(when)(action)

    for copy in small:
        copy.wait()
    picked = [pick_ids[0, d] for d in range(4)]
    one_gain = [None] * LAYERS

    def halo(phase, h, d):
        if phase < LAYERS:
            src, dst, device = outgoing.at[phase, h, d], arrived.at[phase, h, d], ahead[d]
        else:
            layer = 2 * LAYERS - 1 - phase
            src, dst, device = back.at[layer, h, d], returned.at[layer, h, d], behind[d]
        return pltpu.make_async_remote_copy(
            src_ref=src, dst_ref=dst,
            send_sem=send_sem.at[phase, h, d], recv_sem=recv_sem.at[phase, h, d],
            device_id=device, device_id_type=MESH,
        )

    order = (2, 3, 0, 1)

    def start_halo(phase, h):
        for d in order:
            guarded((has_ahead if phase < LAYERS else has_behind)[d], halo(phase, h, d).start)

    def wait_halo(phase, h):
        for d in order:
            guarded((has_behind if phase < LAYERS else has_ahead)[d], halo(phase, h, d).wait_recv)

    def norm(layer, h):
        for b in range(NBLK):
            v = x[layer, h, b]
            r = lax.rsqrt(jnp.mean(v * v, axis=-1, keepdims=True) + EPS)
            unit = v * r
            xhat[layer, h, b] = unit
            scale[layer, h, b] = jnp.broadcast_to(r, (PART, 128))
            xhat16[h, b] = unit.astype(BF16)
            normed[h, b * PART : (b + 1) * PART, :] = (unit * one_gain[layer]).astype(BF16)

    def send(layer, h):
        for d in range(4):
            outgoing[layer, h, d] = xhat16[h, picked[d]]
        start_halo(layer, h)

    def own(layer, h):
        rows = normed[h]
        p_src[h, 0:NBLK] = (0.5 * dot(rows, w_ei[layer, 0:WIDTH, :])).reshape(NBLK, PART, WIDTH)
        p_own[h, :, 0:WIDTH] = 0.5 * dot(rows, w_ei[layer, WIDTH : 2 * WIDTH, :])
        p_own[h, :, WIDTH : 2 * WIDTH] = 0.5 * dot(rows, w_ni[layer, 0:WIDTH, :])

    def finish(layer, h):
        wait_halo(layer, h)
        for d in range(4):
            normed_far[h, d * PART : (d + 1) * PART, :] = (
                arrived[layer, h, d].astype(F32) * one_gain[layer]
            ).astype(BF16)
        p_src[h, NBLK : 2 * NBLK] = (0.5 * dot(normed_far[h], w_ei[layer, 0:WIDTH, :])).reshape(NBLK, PART, WIDTH)
        for c, rows in enumerate(chunks()):
            for b in range(NBLK):
                at = pl.ds(b * PART + c * CHUNK, CHUNK)
                to = p_own[h, at, 0:WIDTH]
                acc = None
                for k in range(SLOTS):
                    e = b * SLOTS + k
                    v, slope = silu_of_half(p_src[h, links[e], rows, :] + to)
                    acc = v if acc is None else acc + v
                    slope_edge[layer, h, e, rows, :] = slope
                edge_sum[h, at, :] = acc.astype(BF16)
        inner = 0.5 * dot(edge_sum[h], w_both[layer]) + p_own[h, :, WIDTH : 2 * WIDTH]
        v, slope = silu_of_half(inner)
        hidden[h] = v.astype(BF16)
        slope_node[layer, h] = 0.5 * slope

    def close(layer, h):
        after = x[layer, h] + dot(hidden[h], w_no[layer]).reshape(NBLK, PART, WIDTH)
        if layer + 1 < LAYERS:
            x[layer + 1, h] = after
        else:
            result[:, pl.ds(h * PART, PART), :] = after

    def flip(layer):
        flip_no[layer] = w_no[layer].T
        flip_both[layer] = w_both[layer].T
        flip_in[layer, 0:WIDTH, :] = w_ei[layer, 0:WIDTH, :].T
        flip_in[layer, WIDTH : 2 * WIDTH, :] = w_ei[layer, WIDTH : 2 * WIDTH, :].T
        flip_in[layer, 2 * WIDTH : 3 * WIDTH, :] = w_ni[layer, 0:WIDTH, :].T

    def pieces():
        return [
            (chains[2 * c + half], rows, pl.ds(half * (WIDTH // 2), WIDTH // 2))
            for c, rows in enumerate(chunks())
            for half in range(2)
        ]

    def back_hidden(layer, h):
        g = grad[:, pl.ds(h * PART, PART), :].reshape(ROWS, WIDTH).astype(BF16)
        d_hidden[h] = dot(g, flip_no[layer])

    def back_far(layer, h):
        if layer < LAYERS - 1:
            back_hidden(layer, h)
        d_inner = (d_hidden[h] * slope_node[layer, h]).astype(BF16)
        d_edge[h] = 0.5 * dot(d_inner, flip_both[layer])
        d_normed[h] = dot(d_inner, flip_in[layer, 2 * WIDTH : 3 * WIDTH, :]).reshape(NBLK, PART, WIDTH)
        for b in range(NBLK):
            acc = [None] * len(chains)
            for k in range(SLOTS):
                e = b * SLOTS + k
                for q, (chain, rows, cols) in enumerate(pieces()):
                    at = pl.ds(b * PART + rows.start, CHUNK)
                    d_pre = d_edge[h, at, cols] * slope_edge[layer, h, e, rows, cols]
                    acc[q] = d_pre if k == 0 else acc[q] + d_pre
                    chain[e] = d_pre + chain[earlier[e]]
            for q, (chain, rows, cols) in enumerate(pieces()):
                at = pl.ds(b * PART + rows.start, CHUNK)
                d_own[h, at, pl.ds(WIDTH + cols.start, cols.size)] = acc[q].astype(BF16)
        for b in range(NBLK):
            for chain, rows, cols in pieces():
                at = pl.ds(b * PART + rows.start, CHUNK)
                d_far[h, at, cols] = chain[last[NBLK + b]].astype(BF16)
                d_own[h, at, cols] = chain[last[b]].astype(BF16)
        d_halo = dot(d_far[h], flip_in[layer, 0:WIDTH, :]).astype(BF16)
        for d in range(4):
            back[layer, h, d] = d_halo[d * PART : (d + 1) * PART, :]

    def back_own(layer, h):
        more = dot(d_own[h], flip_in[layer, 0 : 2 * WIDTH, :]).reshape(NBLK, PART, WIDTH)
        d_normed[h] = d_normed[h] + more

    def gain_terms(layer, h):
        acc = None
        for b in range(NBLK):
            for rows in chunks():
                near = d_normed[h, b, rows, :] * xhat[layer, h, b, rows, :]
                apart = back[layer, h, b, rows, :].astype(F32) * arrived[layer, h, b, rows, :].astype(F32)
                acc = near + apart if acc is None else acc + (near + apart)
        return acc

    def keep_gain(layer, acc):
        acc = jnp.sum(acc, axis=0, keepdims=True)
        for q in range(4):
            gain_mine[layer * 4 + q : layer * 4 + q + 1, :] = acc[:, q * 128 : (q + 1) * 128]

    def back_norm(layer, h):
        wait_halo(2 * LAYERS - 1 - layer, h)
        for c, rows in enumerate(chunks()):
            sent = [returned[layer, h, d, rows, :].astype(F32) for d in range(4)]
            for b in range(NBLK):
                dn = d_normed[h, b, rows, :]
                for d in range(4):
                    dn = dn + chosen[b][d] * sent[d]
                dh = dn * one_gain[layer]
                unit = xhat[layer, h, b, rows, :]
                along = jnp.mean(dh * unit, axis=-1, keepdims=True)
                r = scale[layer, h, b, rows, 0:1]
                at = pl.ds(h * PART + c * CHUNK, CHUNK)
                grad[b, at, :] = grad[b, at, :] + r * (dh - unit * along)

    for layer in range(LAYERS):
        one_gain[layer] = 1.0 + gain[layer : layer + 1, :]
    load_x[0].wait()
    norm(0, 0)
    pl.semaphore_wait(barrier, 4 + len(near) + len(far))
    send(0, 0)
    for h in range(1, STREAMS):
        load_x[h].wait()
        norm(0, h)
        send(0, h)
    for copy in weights[0][:2]:
        copy.wait()
    for h in range(STREAMS):
        own(0, h)

    zeros = jnp.zeros((PART, WIDTH), BF16)
    for d in (2, 3):

        def clear_arrived(d=d):
            for layer in range(LAYERS):
                for h in range(STREAMS):
                    arrived[layer, h, d] = zeros

        def clear_returned(d=d):
            for layer in range(LAYERS):
                for h in range(STREAMS):
                    returned[layer, h, d] = zeros

        pl.when(jnp.logical_not(has_behind[d]))(clear_arrived)
        pl.when(jnp.logical_not(has_ahead[d]))(clear_returned)
    for chain in chains:
        chain[EDGES] = jnp.zeros((CHUNK, WIDTH // 2), F32)

    links = [send_ids[e // SLOTS, e % SLOTS] for e in range(EDGES)]
    chosen = [[same(picked[d], b).astype(F32) for d in range(4)] for b in range(NBLK)]

    earlier = []
    for e in range(EDGES):
        found = jnp.int32(EDGES)
        for f in range(e):
            found = found + same(links[f], links[e]) * (f - found)
        earlier.append(found)
    last = []
    for s in range(2 * NBLK):
        found = jnp.int32(EDGES)
        for f in range(EDGES):
            found = found + same(links[f], s) * (f - found)
        last.append(found)

    for copy in weights[0][2:] + weights[1]:
        copy.wait()
    for layer in range(LAYERS):
        w_both[layer] = dot(w_eo[layer], w_ni[layer, WIDTH : 2 * WIDTH, :]).astype(BF16)
    flip(1)

    for layer in range(LAYERS - 1):
        for h in range(STREAMS):
            finish(layer, h)
            close(layer, h)
            norm(layer + 1, h)
            send(layer + 1, h)
        for h in range(STREAMS):
            own(layer + 1, h)
        flip(layer)
    load_g.wait()
    for h in range(STREAMS):
        back_hidden(LAYERS - 1, h)
    for h in range(STREAMS):
        finish(LAYERS - 1, h)
        back_far(LAYERS - 1, h)
        start_halo(LAYERS, h)

    for layer in reversed(range(LAYERS)):
        terms = None
        if layer == LAYERS - 1:
            for h in range(STREAMS):
                close(layer, h)
                back_own(layer, h)
                more = gain_terms(layer, h)
                terms = more if terms is None else terms + more
            keep_gain(layer, terms)
            continue
        for h in range(STREAMS):
            back_norm(layer + 1, h)
            back_far(layer, h)
            if layer > 0 or h < STREAMS - 1:
                start_halo(2 * LAYERS - 1 - layer, h)
            back_own(layer, h)
            more = gain_terms(layer, h)
            terms = more if terms is None else terms + more
        keep_gain(layer, terms)

    def near_copy(t):
        return pltpu.make_async_remote_copy(
            src_ref=gain_mine, dst_ref=gather_near.at[near_slot], send_sem=ar_send.at[0], recv_sem=ar_recv.at[0],
            device_id=near[t], device_id_type=MESH,
        )

    def far_copy(t):
        return pltpu.make_async_remote_copy(
            src_ref=gain_near, dst_ref=gather_far.at[far_slot], send_sem=ar_send.at[1], recv_sem=ar_recv.at[1],
            device_id=far[t], device_id_type=MESH,
        )

    def all_of(gather, n, sem):
        return pltpu.make_async_copy(gather.at[pl.ds(0, n)], gather.at[pl.ds(0, n)], sem)

    for t in range(len(near)):
        near_copy(t).start()
    start_halo(2 * LAYERS - 1, STREAMS - 1)
    gather_near[near_slot] = gain_mine[...]

    for h in range(STREAMS - 1):
        back_norm(0, h)
    all_of(gather_near, len(near), ar_recv.at[0]).wait()
    part = gather_near[0]
    for t in range(1, len(near) + 1):
        part = part + gather_near[t]
    gain_near[...] = part
    for t in range(len(far)):
        far_copy(t).start()
    gather_far[far_slot] = part
    back_norm(0, STREAMS - 1)
    for phase in range(2 * LAYERS):
        for h in range(STREAMS):
            for d in range(4):
                guarded((has_ahead if phase < LAYERS else has_behind)[d], halo(phase, h, d).wait_send)
    all_of(gather_near, len(near), ar_send.at[0]).wait()
    all_of(gather_far, len(far), ar_recv.at[1]).wait()
    whole = gather_far[0]
    for t in range(1, len(far) + 1):
        whole = whole + gather_far[t]
    for layer in range(LAYERS):
        for q in range(4):
            grad_gains[layer : layer + 1, q * 128 : (q + 1) * 128] = whole[layer * 4 + q : layer * 4 + q + 1, :]
    all_of(gather_far, len(far), ar_send.at[1]).wait()


def hand_over(result, grad_state, grad_gains, result_out, grad_out, gains_out, sem):
    copies = [pltpu.make_async_copy(grad_gains, gains_out, sem.at[2 * NBLK])]
    for b in range(NBLK):
        copies.append(pltpu.make_async_copy(result.at[b], result_out.at[b], sem.at[b]))
        copies.append(pltpu.make_async_copy(grad_state.at[b], grad_out.at[b], sem.at[NBLK + b]))
    for copy in copies:
        copy.start()
    for copy in copies:
        copy.wait()


def solution(mesh):
    n_lon, n_lat = mesh.shape["lon"], mesh.shape["lat"]

    def local(state, cotangent, gains, senders, halo_map, edge_in, edge_out, node_in, node_out):
        outside = pl.BlockSpec(memory_space=pltpu.HBM)
        vmem = pltpu.VMEM
        whole = (NBLK, BLOCK, WIDTH)
        split_rows = (STREAMS, NBLK, PART, WIDTH)
        flat = (STREAMS, ROWS, WIDTH)
        halos = (LAYERS, STREAMS, 4, PART, WIDTH)
        scratch = [
            vmem((LAYERS,) + split_rows, F32),
            vmem((LAYERS, WIDTH), F32),
            pltpu.SMEM((NBLK, SLOTS), jnp.int32),
            pltpu.SMEM((1, 4), jnp.int32),
            vmem((LAYERS, 2 * WIDTH, WIDTH), BF16),
            vmem((LAYERS, WIDTH, WIDTH), BF16),
            vmem((LAYERS, 2 * WIDTH, WIDTH), BF16),
            vmem((LAYERS, WIDTH, WIDTH), BF16),
            vmem((LAYERS, WIDTH, WIDTH), BF16),
            vmem((LAYERS, WIDTH, WIDTH), BF16),
            vmem((LAYERS, WIDTH, WIDTH), BF16),
            vmem((LAYERS, 3 * WIDTH, WIDTH), BF16),
            vmem((LAYERS,) + split_rows, F32),
            vmem((LAYERS, STREAMS, NBLK, PART, 128), F32),
            vmem(split_rows, BF16),
            vmem(flat, BF16),
            vmem(halos, BF16),
            vmem(halos, BF16),
            vmem(flat, BF16),
            vmem((STREAMS, 2 * NBLK, PART, WIDTH), F32),
            vmem((STREAMS, ROWS, 2 * WIDTH), F32),
            vmem((LAYERS, STREAMS, EDGES, PART, WIDTH), F32),
            vmem((LAYERS,) + flat, F32),
            vmem(flat, BF16),
            vmem(flat, BF16),
            vmem(flat, F32),
            vmem(flat, F32),
            [vmem((EDGES + 1, CHUNK, WIDTH // 2), F32)] * (2 * (PART // CHUNK)),
            vmem((STREAMS, ROWS, 2 * WIDTH), BF16),
            vmem(flat, BF16),
            vmem(halos, BF16),
            vmem(halos, BF16),
            vmem(split_rows, F32),
            vmem((8, 128), F32),
            vmem((8, 128), F32),
            vmem((n_lat, 8, 128), F32),
            vmem((n_lon, 8, 128), F32),
            pltpu.SemaphoreType.DMA((4 + STREAMS,)),
            pltpu.SemaphoreType.DMA((LAYERS, 4)),
            pltpu.SemaphoreType.DMA((2 * LAYERS, STREAMS, 4)),
            pltpu.SemaphoreType.DMA((2 * LAYERS, STREAMS, 4)),
            pltpu.SemaphoreType.DMA((2,)),
            pltpu.SemaphoreType.DMA((2,)),
        ]
        result, grad_state, grad_gains = pl.pallas_call(
            lambda *refs: kernel(n_lon, n_lat, *refs),
            out_shape=(vmem(whole, F32), vmem(whole, F32), vmem((LAYERS, WIDTH), F32)),
            in_specs=[outside] * 9,
            scratch_shapes=scratch,
            compiler_params=pltpu.CompilerParams(
                collective_id=0, has_side_effects=True, vmem_limit_bytes=60 * 2**20
            ),
            cost_estimate=pl.CostEstimate(flops=4 * 10**9, bytes_accessed=10**7, transcendentals=2 * 10**6),
            name="mesh_steps",
        )(
            state.reshape(whole),
            cotangent.reshape(whole),
            gains,
            senders.reshape(NBLK, SLOTS),
            halo_map.reshape(1, 4),
            edge_in,
            edge_out,
            node_in,
            node_out,
        )
        result, grad_state, grad_gains = pl.pallas_call(
            hand_over,
            out_shape=(
                jax.ShapeDtypeStruct(whole, F32),
                jax.ShapeDtypeStruct(whole, F32),
                jax.ShapeDtypeStruct((LAYERS, WIDTH), F32),
            ),
            in_specs=[pl.BlockSpec(memory_space=pl.ANY)] * 3,
            out_specs=(outside,) * 3,
            scratch_shapes=[pltpu.SemaphoreType.DMA((2 * NBLK + 1,))],
            compiler_params=pltpu.CompilerParams(vmem_limit_bytes=2**20),
            name="hand_over",
        )(result, grad_state, grad_gains)
        shape = (1, 1, NBLK * BLOCK, WIDTH)
        return result.reshape(shape), grad_state.reshape(shape), grad_gains

    split = P("lon", "lat", None, None)
    return jax.shard_map(
        local,
        mesh=mesh,
        in_specs=(split, split, P(), split, split, P(), P(), P(), P()),
        out_specs=(split, split, P()),
        check_vma=False,
    )
```

```python
import jax
import jax.numpy as jnp
from jax import lax
from jax.experimental import pallas as pl
from jax.experimental.pallas import tpu as pltpu
from jax.sharding import PartitionSpec as P

MESH = pl.DeviceIdType.MESH
F32 = jnp.float32
BF16 = jnp.bfloat16
LAYERS = 2
NBLK = 4
SLOTS = 4
BLOCK = 64
WIDTH = 512
EDGES = NBLK * SLOTS
STREAMS = 2
PART = BLOCK // STREAMS
ROWS = NBLK * PART
CHUNK = 16
EPS = 1e-06


def dot(a, b):
    return jnp.dot(a, b, preferred_element_type=F32)


def same(a, b):
    apart = a - b
    return 1 - jnp.minimum(apart * apart, 1)


def silu_of_half(v):
    u = 1.0 + jnp.tanh(v)
    out = v * u
    return out, u + out * (2.0 - u)


def chunks():
    return [pl.ds(c * CHUNK, CHUNK) for c in range(PART // CHUNK)]


def kernel(
    n_lon, n_lat,
    state, cotangent, gains, senders, picks, edge_in, edge_out, node_in, node_out,
    result, grad, grad_gains,
    x, gain, send_ids, pick_ids, w_ei, w_eo, w_ni, w_no, w_both, flip_no, flip_both, flip_in,
    xhat, scale, xhat16, normed, outgoing, arrived, normed_far, p_src, p_own,
    slope_edge, slope_node, edge_sum, hidden, d_hidden, d_edge,
    chains, d_own, d_far, back, returned, d_normed,
    gain_mine, gain_near, gather_near, gather_far,
    load_sem, weight_sem, send_sem, recv_sem, ar_send, ar_recv, heard, heard_across,
):
    i = lax.axis_index("lon")
    j = lax.axis_index("lat")
    east, west = lax.rem(i + 1, n_lon), lax.rem(i + n_lon - 1, n_lon)
    north, south = lax.rem(j + 1, n_lat), lax.rem(j + n_lat - 1, n_lat)
    ahead = ((east, j), (west, j), (i, north), (i, south))
    behind = ((west, j), (east, j), (i, south), (i, north))
    has_ahead = (None, None, j < n_lat - 1, j > 0)
    has_behind = (None, None, j > 0, j < n_lat - 1)

    small = [
        pltpu.make_async_copy(picks, pick_ids, load_sem.at[0]),
        pltpu.make_async_copy(senders, send_ids, load_sem.at[1]),
        pltpu.make_async_copy(gains, gain, load_sem.at[2]),
    ]
    load_x = [
        pltpu.make_async_copy(state.at[:, pl.ds(h * PART, PART), :], x.at[0, h], load_sem.at[3 + h])
        for h in range(STREAMS)
    ]
    load_g = pltpu.make_async_copy(cotangent, grad, load_sem.at[3 + STREAMS])
    weights = [
        [
            pltpu.make_async_copy(full.at[layer], held.at[layer], weight_sem.at[layer, n])
            for n, (full, held) in enumerate(
                ((edge_in, w_ei), (node_in, w_ni), (edge_out, w_eo), (node_out, w_no))
            )
        ]
        for layer in range(LAYERS)
    ]
    for copy in small + load_x:
        copy.start()

    barrier = pltpu.get_barrier_semaphore()

    depth, columns = n_lat // 2, n_lon // 2
    core, column, high, z = i % 2, i // 2, j // depth, j % depth
    near_slot, far_slot = core * depth + z, column * 2 + high
    apart = lambda t, n: min(t, n - t)
    near = [
        (column * 2 + (core + c) % 2, high * depth + (z + t) % depth)
        for t in sorted(range(depth), key=lambda t: -apart(t, depth)) for c in range(2) if c + t > 0
    ]
    far = [
        ((column + t) % columns * 2 + core, (high + c) % 2 * depth + z)
        for c in (1, 0) for t in sorted(range(columns), key=lambda t: -apart(t, columns)) if c + t > 0
    ]
    for device in ahead:
        pl.semaphore_signal(barrier, inc=1, device_id=device, device_id_type=MESH)
    for layer in range(LAYERS):
        for copy in weights[layer]:
            copy.start()
    load_g.start()

    def guarded(when, action):
        if when is None:
            action()
        else:
            pl.when(when)(action)

    for copy in small:
        copy.wait()
    picked = [pick_ids[0, d] for d in range(4)]
    one_gain = [None] * LAYERS

    def halo(phase, h, d):
        if phase < LAYERS:
            src, dst, device = outgoing.at[phase, h, d], arrived.at[phase, h, d], ahead[d]
        else:
            layer = 2 * LAYERS - 1 - phase
            src, dst, device = back.at[layer, h, d], returned.at[layer, h, d], behind[d]
        return pltpu.make_async_remote_copy(
            src_ref=src, dst_ref=dst,
            send_sem=send_sem.at[phase, h, d], recv_sem=recv_sem.at[phase, h, d],
            device_id=device, device_id_type=MESH,
        )

    order = (2, 3, 0, 1)

    def start_halo(phase, h):
        for d in order:
            guarded((has_ahead if phase < LAYERS else has_behind)[d], halo(phase, h, d).start)

    def wait_halo(phase, h):
        for d in order:
            guarded((has_behind if phase < LAYERS else has_ahead)[d], halo(phase, h, d).wait_recv)

    def norm(layer, h):
        for b in range(NBLK):
            v = x[layer, h, b]
            r = lax.rsqrt(jnp.mean(v * v, axis=-1, keepdims=True) + EPS)
            unit = v * r
            xhat[layer, h, b] = unit
            scale[layer, h, b] = jnp.broadcast_to(r, (PART, 128))
            xhat16[h, b] = unit.astype(BF16)
            normed[h, b * PART : (b + 1) * PART, :] = (unit * one_gain[layer]).astype(BF16)

    def send(layer, h):
        for d in range(4):
            outgoing[layer, h, d] = xhat16[h, picked[d]]
        start_halo(layer, h)

    def own(layer, h):
        rows = normed[h]
        p_src[h, 0:NBLK] = (0.5 * dot(rows, w_ei[layer, 0:WIDTH, :])).reshape(NBLK, PART, WIDTH)
        p_own[h, :, 0:WIDTH] = 0.5 * dot(rows, w_ei[layer, WIDTH : 2 * WIDTH, :])
        p_own[h, :, WIDTH : 2 * WIDTH] = 0.5 * dot(rows, w_ni[layer, 0:WIDTH, :])

    def finish(layer, h):
        wait_halo(layer, h)
        for d in range(4):
            normed_far[h, d * PART : (d + 1) * PART, :] = (
                arrived[layer, h, d].astype(F32) * one_gain[layer]
            ).astype(BF16)
        p_src[h, NBLK : 2 * NBLK] = (0.5 * dot(normed_far[h], w_ei[layer, 0:WIDTH, :])).reshape(NBLK, PART, WIDTH)
        for c, rows in enumerate(chunks()):
            for b in range(NBLK):
                at = pl.ds(b * PART + c * CHUNK, CHUNK)
                to = p_own[h, at, 0:WIDTH]
                acc = None
                for k in range(SLOTS):
                    e = b * SLOTS + k
                    v, slope = silu_of_half(p_src[h, links[e], rows, :] + to)
                    acc = v if acc is None else acc + v
                    slope_edge[layer, h, e, rows, :] = slope
                edge_sum[h, at, :] = acc.astype(BF16)
        inner = 0.5 * dot(edge_sum[h], w_both[layer]) + p_own[h, :, WIDTH : 2 * WIDTH]
        v, slope = silu_of_half(inner)
        hidden[h] = v.astype(BF16)
        slope_node[layer, h] = 0.5 * slope

    def close(layer, h):
        after = x[layer, h] + dot(hidden[h], w_no[layer]).reshape(NBLK, PART, WIDTH)
        if layer + 1 < LAYERS:
            x[layer + 1, h] = after
        else:
            result[:, pl.ds(h * PART, PART), :] = after

    def flip(layer):
        flip_no[layer] = w_no[layer].T
        flip_both[layer] = w_both[layer].T
        flip_in[layer, 0:WIDTH, :] = w_ei[layer, 0:WIDTH, :].T
        flip_in[layer, WIDTH : 2 * WIDTH, :] = w_ei[layer, WIDTH : 2 * WIDTH, :].T
        flip_in[layer, 2 * WIDTH : 3 * WIDTH, :] = w_ni[layer, 0:WIDTH, :].T

    def pieces():
        return [
            (chains[2 * c + half], rows, pl.ds(half * (WIDTH // 2), WIDTH // 2))
            for c, rows in enumerate(chunks())
            for half in range(2)
        ]

    def back_hidden(layer, h):
        g = grad[:, pl.ds(h * PART, PART), :].reshape(ROWS, WIDTH).astype(BF16)
        d_hidden[h] = dot(g, flip_no[layer])

    def back_far(layer, h):
        if layer < LAYERS - 1:
            back_hidden(layer, h)
        d_inner = (d_hidden[h] * slope_node[layer, h]).astype(BF16)
        d_edge[h] = 0.5 * dot(d_inner, flip_both[layer])
        d_normed[h] = dot(d_inner, flip_in[layer, 2 * WIDTH : 3 * WIDTH, :]).reshape(NBLK, PART, WIDTH)
        for b in range(NBLK):
            acc = [None] * len(chains)
            for k in range(SLOTS):
                e = b * SLOTS + k
                for q, (chain, rows, cols) in enumerate(pieces()):
                    at = pl.ds(b * PART + rows.start, CHUNK)
                    d_pre = d_edge[h, at, cols] * slope_edge[layer, h, e, rows, cols]
                    acc[q] = d_pre if k == 0 else acc[q] + d_pre
                    chain[e] = d_pre + chain[earlier[e]]
            for q, (chain, rows, cols) in enumerate(pieces()):
                at = pl.ds(b * PART + rows.start, CHUNK)
                d_own[h, at, pl.ds(WIDTH + cols.start, cols.size)] = acc[q].astype(BF16)
        for b in range(NBLK):
            for chain, rows, cols in pieces():
                at = pl.ds(b * PART + rows.start, CHUNK)
                d_far[h, at, cols] = chain[last[NBLK + b]].astype(BF16)
                d_own[h, at, cols] = chain[last[b]].astype(BF16)
        d_halo = dot(d_far[h], flip_in[layer, 0:WIDTH, :]).astype(BF16)
        for d in range(4):
            back[layer, h, d] = d_halo[d * PART : (d + 1) * PART, :]

    def back_own(layer, h):
        more = dot(d_own[h], flip_in[layer, 0 : 2 * WIDTH, :]).reshape(NBLK, PART, WIDTH)
        d_normed[h] = d_normed[h] + more

    def gain_terms(layer, h):
        acc = None
        for b in range(NBLK):
            for rows in chunks():
                near = d_normed[h, b, rows, :] * xhat[layer, h, b, rows, :]
                apart = back[layer, h, b, rows, :].astype(F32) * arrived[layer, h, b, rows, :].astype(F32)
                acc = near + apart if acc is None else acc + (near + apart)
        return acc

    def keep_gain(layer, acc):
        acc = jnp.sum(acc, axis=0, keepdims=True)
        for q in range(4):
            gain_mine[layer * 4 + q : layer * 4 + q + 1, :] = acc[:, q * 128 : (q + 1) * 128]

    def back_norm(layer, h):
        wait_halo(2 * LAYERS - 1 - layer, h)
        for c, rows in enumerate(chunks()):
            sent = [returned[layer, h, d, rows, :].astype(F32) for d in range(4)]
            for b in range(NBLK):
                dn = d_normed[h, b, rows, :]
                for d in range(4):
                    dn = dn + chosen[b][d] * sent[d]
                dh = dn * one_gain[layer]
                unit = xhat[layer, h, b, rows, :]
                along = jnp.mean(dh * unit, axis=-1, keepdims=True)
                r = scale[layer, h, b, rows, 0:1]
                at = pl.ds(h * PART + c * CHUNK, CHUNK)
                grad[b, at, :] = grad[b, at, :] + r * (dh - unit * along)

    steps = (2, 4)

    def tell(r):
        step = steps[r]
        if step % n_lon:
            for d, to in ((0, lax.rem(i + step, n_lon)), (1, lax.rem(i + n_lon - step % n_lon, n_lon))):
                pl.semaphore_signal(heard.at[r, d], inc=1, device_id=(to, j), device_id_type=MESH)
        for d, to, there in ((2, j + step, j + step < n_lat), (3, j - step, j >= step)):

            def say(d=d, to=to):
                pl.semaphore_signal(heard.at[r, d], inc=1, device_id=(i, to), device_id_type=MESH)

            pl.when(there)(say)

    def hear(r):
        step = steps[r]
        if step % n_lon:
            for d in (0, 1):
                pl.semaphore_wait(heard.at[r, d], 1)
        for d, there in ((2, j >= step), (3, j + step < n_lat)):
            pl.when(there)(lambda d=d: pl.semaphore_wait(heard.at[r, d], 1))

    for layer in range(LAYERS):
        one_gain[layer] = 1.0 + gain[layer : layer + 1, :]
    load_x[0].wait()
    norm(0, 0)
    pl.semaphore_wait(barrier, 4)
    send(0, 0)
    for h in range(1, STREAMS):
        load_x[h].wait()
        norm(0, h)
        send(0, h)
    for copy in weights[0][:2]:
        copy.wait()
    for h in range(STREAMS):
        own(0, h)

    zeros = jnp.zeros((PART, WIDTH), BF16)
    for d in (2, 3):

        def clear_arrived(d=d):
            for layer in range(LAYERS):
                for h in range(STREAMS):
                    arrived[layer, h, d] = zeros

        def clear_returned(d=d):
            for layer in range(LAYERS):
                for h in range(STREAMS):
                    returned[layer, h, d] = zeros

        pl.when(jnp.logical_not(has_behind[d]))(clear_arrived)
        pl.when(jnp.logical_not(has_ahead[d]))(clear_returned)
    for chain in chains:
        chain[EDGES] = jnp.zeros((CHUNK, WIDTH // 2), F32)

    links = [send_ids[e // SLOTS, e % SLOTS] for e in range(EDGES)]
    chosen = [[same(picked[d], b).astype(F32) for d in range(4)] for b in range(NBLK)]

    earlier = []
    for e in range(EDGES):
        found = jnp.int32(EDGES)
        for f in range(e):
            found = found + same(links[f], links[e]) * (f - found)
        earlier.append(found)
    last = []
    for s in range(2 * NBLK):
        found = jnp.int32(EDGES)
        for f in range(EDGES):
            found = found + same(links[f], s) * (f - found)
        last.append(found)

    for copy in weights[0][2:] + weights[1]:
        copy.wait()
    for layer in range(LAYERS):
        w_both[layer] = dot(w_eo[layer], w_ni[layer, WIDTH : 2 * WIDTH, :]).astype(BF16)
    flip(1)

    for layer in range(LAYERS - 1):
        for h in range(STREAMS):
            finish(layer, h)
            close(layer, h)
            norm(layer + 1, h)
            send(layer + 1, h)
            if layer == 0 and h == 0:
                tell(0)
        for h in range(STREAMS):
            own(layer + 1, h)
        flip(layer)
    load_g.wait()
    for h in range(STREAMS):
        back_hidden(LAYERS - 1, h)
    for h in range(STREAMS):
        finish(LAYERS - 1, h)
        back_far(LAYERS - 1, h)
        start_halo(LAYERS, h)
        if h == 0:
            hear(0)
            tell(1)

    for layer in reversed(range(LAYERS)):
        terms = None
        if layer == LAYERS - 1:
            for h in range(STREAMS):
                close(layer, h)
                back_own(layer, h)
                more = gain_terms(layer, h)
                terms = more if terms is None else terms + more
            keep_gain(layer, terms)
            continue
        for h in range(STREAMS):
            back_norm(layer + 1, h)
            back_far(layer, h)
            if layer > 0 or h < STREAMS - 1:
                start_halo(2 * LAYERS - 1 - layer, h)
            if layer == 0 and h == 0:
                hear(1)
                pl.semaphore_signal(
                    heard_across, inc=1, device_id=(i, lax.rem(j + depth, n_lat)), device_id_type=MESH
                )
            back_own(layer, h)
            more = gain_terms(layer, h)
            terms = more if terms is None else terms + more
        keep_gain(layer, terms)

    def near_copy(t):
        return pltpu.make_async_remote_copy(
            src_ref=gain_mine, dst_ref=gather_near.at[near_slot], send_sem=ar_send.at[0], recv_sem=ar_recv.at[0],
            device_id=near[t], device_id_type=MESH,
        )

    def far_copy(t):
        return pltpu.make_async_remote_copy(
            src_ref=gain_near, dst_ref=gather_far.at[far_slot], send_sem=ar_send.at[1], recv_sem=ar_recv.at[1],
            device_id=far[t], device_id_type=MESH,
        )

    def all_of(gather, n, sem):
        return pltpu.make_async_copy(gather.at[pl.ds(0, n)], gather.at[pl.ds(0, n)], sem)

    for t in range(len(near)):
        near_copy(t).start()
    start_halo(2 * LAYERS - 1, STREAMS - 1)
    gather_near[near_slot] = gain_mine[...]

    for h in range(STREAMS - 1):
        back_norm(0, h)
    all_of(gather_near, len(near), ar_recv.at[0]).wait()
    part = gather_near[0]
    for t in range(1, len(near) + 1):
        part = part + gather_near[t]
    gain_near[...] = part
    pl.semaphore_wait(heard_across, 1)
    for t in range(len(far)):
        far_copy(t).start()
    gather_far[far_slot] = part
    back_norm(0, STREAMS - 1)
    for phase in range(2 * LAYERS):
        for h in range(STREAMS):
            for d in range(4):
                guarded((has_ahead if phase < LAYERS else has_behind)[d], halo(phase, h, d).wait_send)
    all_of(gather_near, len(near), ar_send.at[0]).wait()
    all_of(gather_far, len(far), ar_recv.at[1]).wait()
    whole = gather_far[0]
    for t in range(1, len(far) + 1):
        whole = whole + gather_far[t]
    for layer in range(LAYERS):
        for q in range(4):
            grad_gains[layer : layer + 1, q * 128 : (q + 1) * 128] = whole[layer * 4 + q : layer * 4 + q + 1, :]
    all_of(gather_far, len(far), ar_send.at[1]).wait()


def hand_over(result, grad_state, grad_gains, result_out, grad_out, gains_out, sem):
    copies = [pltpu.make_async_copy(grad_gains, gains_out, sem.at[2 * NBLK])]
    for b in range(NBLK):
        copies.append(pltpu.make_async_copy(result.at[b], result_out.at[b], sem.at[b]))
        copies.append(pltpu.make_async_copy(grad_state.at[b], grad_out.at[b], sem.at[NBLK + b]))
    for copy in copies:
        copy.start()
    for copy in copies:
        copy.wait()


def solution(mesh):
    n_lon, n_lat = mesh.shape["lon"], mesh.shape["lat"]

    def local(state, cotangent, gains, senders, halo_map, edge_in, edge_out, node_in, node_out):
        outside = pl.BlockSpec(memory_space=pltpu.HBM)
        vmem = pltpu.VMEM
        whole = (NBLK, BLOCK, WIDTH)
        split_rows = (STREAMS, NBLK, PART, WIDTH)
        flat = (STREAMS, ROWS, WIDTH)
        halos = (LAYERS, STREAMS, 4, PART, WIDTH)
        scratch = [
            vmem((LAYERS,) + split_rows, F32),
            vmem((LAYERS, WIDTH), F32),
            pltpu.SMEM((NBLK, SLOTS), jnp.int32),
            pltpu.SMEM((1, 4), jnp.int32),
            vmem((LAYERS, 2 * WIDTH, WIDTH), BF16),
            vmem((LAYERS, WIDTH, WIDTH), BF16),
            vmem((LAYERS, 2 * WIDTH, WIDTH), BF16),
            vmem((LAYERS, WIDTH, WIDTH), BF16),
            vmem((LAYERS, WIDTH, WIDTH), BF16),
            vmem((LAYERS, WIDTH, WIDTH), BF16),
            vmem((LAYERS, WIDTH, WIDTH), BF16),
            vmem((LAYERS, 3 * WIDTH, WIDTH), BF16),
            vmem((LAYERS,) + split_rows, F32),
            vmem((LAYERS, STREAMS, NBLK, PART, 128), F32),
            vmem(split_rows, BF16),
            vmem(flat, BF16),
            vmem(halos, BF16),
            vmem(halos, BF16),
            vmem(flat, BF16),
            vmem((STREAMS, 2 * NBLK, PART, WIDTH), F32),
            vmem((STREAMS, ROWS, 2 * WIDTH), F32),
            vmem((LAYERS, STREAMS, EDGES, PART, WIDTH), F32),
            vmem((LAYERS,) + flat, F32),
            vmem(flat, BF16),
            vmem(flat, BF16),
            vmem(flat, F32),
            vmem(flat, F32),
            [vmem((EDGES + 1, CHUNK, WIDTH // 2), F32)] * (2 * (PART // CHUNK)),
            vmem((STREAMS, ROWS, 2 * WIDTH), BF16),
            vmem(flat, BF16),
            vmem(halos, BF16),
            vmem(halos, BF16),
            vmem(split_rows, F32),
            vmem((8, 128), F32),
            vmem((8, 128), F32),
            vmem((n_lat, 8, 128), F32),
            vmem((n_lon, 8, 128), F32),
            pltpu.SemaphoreType.DMA((4 + STREAMS,)),
            pltpu.SemaphoreType.DMA((LAYERS, 4)),
            pltpu.SemaphoreType.DMA((2 * LAYERS, STREAMS, 4)),
            pltpu.SemaphoreType.DMA((2 * LAYERS, STREAMS, 4)),
            pltpu.SemaphoreType.DMA((2,)),
            pltpu.SemaphoreType.DMA((2,)),
            pltpu.SemaphoreType.REGULAR((2, 4)),
            pltpu.SemaphoreType.REGULAR,
        ]
        result, grad_state, grad_gains = pl.pallas_call(
            lambda *refs: kernel(n_lon, n_lat, *refs),
            out_shape=(vmem(whole, F32), vmem(whole, F32), vmem((LAYERS, WIDTH), F32)),
            in_specs=[outside] * 9,
            scratch_shapes=scratch,
            compiler_params=pltpu.CompilerParams(
                collective_id=0, has_side_effects=True, vmem_limit_bytes=60 * 2**20
            ),
            cost_estimate=pl.CostEstimate(flops=4 * 10**9, bytes_accessed=10**7, transcendentals=2 * 10**6),
            name="mesh_steps",
        )(
            state.reshape(whole),
            cotangent.reshape(whole),
            gains,
            senders.reshape(NBLK, SLOTS),
            halo_map.reshape(1, 4),
            edge_in,
            edge_out,
            node_in,
            node_out,
        )
        result, grad_state, grad_gains = pl.pallas_call(
            hand_over,
            out_shape=(
                jax.ShapeDtypeStruct(whole, F32),
                jax.ShapeDtypeStruct(whole, F32),
                jax.ShapeDtypeStruct((LAYERS, WIDTH), F32),
            ),
            in_specs=[pl.BlockSpec(memory_space=pl.ANY)] * 3,
            out_specs=(outside,) * 3,
            scratch_shapes=[pltpu.SemaphoreType.DMA((2 * NBLK + 1,))],
            compiler_params=pltpu.CompilerParams(vmem_limit_bytes=2**20),
            name="hand_over",
        )(result, grad_state, grad_gains)
        shape = (1, 1, NBLK * BLOCK, WIDTH)
        return result.reshape(shape), grad_state.reshape(shape), grad_gains

    split = P("lon", "lat", None, None)
    return jax.shard_map(
        local,
        mesh=mesh,
        in_specs=(split, split, P(), split, split, P(), P(), P(), P()),
        out_specs=(split, split, P()),
        check_vma=False,
    )
```
